32 devices in a mesh: rows: 8 (over z, y), rep: 4 (over x, core).
Axes of the slice: x: 2, y: 2, z: 4, core: 2. Of those that a mesh axis runs over, the one named last changes fastest.
Arguments:
- features: bfloat16 [32768, 256], P(('rows', 'rep')), may hold values from -6 to 6
- weight: bfloat16 [256, 256], replicated, may hold values from -0.375 to 0.375
- block_cols: int32 [256, 4, 2], P('rows', 'rep'), may hold values from 0 to 63, as said below
- block_vals: bfloat16 [256, 4, 2, 128, 128], P('rows', 'rep'), as said below
- out_grad: bfloat16 [32768, 256], P('rows'), may hold values from -6 to 6
Outputs:
- activations: bfloat16 [32768, 256], P(('rows', 'rep'))
- input_grad: bfloat16 [32768, 256], P(('rows', 'rep'))
- weight_grad: float32 [256, 256], replicated
The draws below stay inside these ranges and needn't reach their ends.
Inputs may be any that keep to these rules, and one draw needn't show every extreme that they name: `block_cols`: layer c's k-th block column is global block column (k // 8) * 32 + c * 8 + k % 8, whose rows the device of index k // 8 along rows holds in layer c. In the layer that owns a block row, slot 0 is its diagonal block; no other held block of a device lies in its own block columns. For every layer, every device along rows and every other device along rows, at most 10 of the first device's held blocks in that layer lie in block columns of the other, and in every draw some pair has exactly 10. `block_vals`: the adjacency is symmetric: every held block at block row b, block column g in slot s has a partner held at block row g, block column b in slot s (of the layer owning b) that is its transpose; diagonal blocks are symmetric.
All inputs are finite; a program needn't handle non-finite values.
Results may differ from the reference program's by a relative error of at most 0.006.
Values may be sent and summed in bfloat16 or wider, within the bound.
No kernel may reach another device: no remote copies, remote signals or barrier semaphores. Data moves between devices by JAX's collectives and lax.ppermute only.
A program may use at most 128 MiB of HBM per device.

```python
import math
import jax
import jax.numpy as jnp
from jax import lax

WIDTH = 256
BLOCK = 128
SLOTS = 2
ROW_BLOCKS = 32
OWN_BLOCKS = 8
BLOCKS = 256
NODES = 32768
N_ROWS = 8
N_REP = 4


def block_layout(base_key):
    group_count = N_ROWS
    class_count = N_ROWS // 2 - 1
    couple_count = SLOTS * OWN_BLOCKS // 2
    rotation_order = jax.random.permutation(jax.random.fold_in(base_key, 71), group_count).astype(jnp.int32)
    rotation_place = jnp.zeros_like(rotation_order).at[rotation_order].set(jnp.arange(group_count, dtype=jnp.int32))
    shuffle = jax.random.permutation(jax.random.fold_in(base_key, 72), class_count).astype(jnp.int32)
    full_shape = (BLOCKS, N_REP, SLOTS)
    blocks = jnp.arange(BLOCKS, dtype=jnp.int32)[:, None, None]
    home_group = jnp.broadcast_to(blocks // ROW_BLOCKS, full_shape)
    home_class = jnp.broadcast_to(blocks % ROW_BLOCKS // OWN_BLOCKS, full_shape)
    home_place = jnp.broadcast_to(blocks % OWN_BLOCKS, full_shape)
    layer_ids = jnp.broadcast_to(jnp.arange(N_REP, dtype=jnp.int32)[None, :, None], full_shape)
    slot_index = jnp.broadcast_to(jnp.arange(SLOTS, dtype=jnp.int32)[None, None, :], full_shape)
    own_layer = layer_ids == home_class
    item_index = slot_index * OWN_BLOCKS + home_place
    pair_running = (jnp.bitwise_xor(home_class, layer_ids) - 1) * couple_count + item_index // 2
    own_running = (N_REP - 1) * couple_count + home_place // 2
    running = jnp.where(own_layer, own_running, pair_running)
    offset_size = 1 + shuffle[running % class_count]
    parity = jnp.where(jnp.where(own_layer, home_place, item_index) % 2 == 0, 1, -1)
    direction = jnp.where(layer_ids > home_class, 1, -1)
    offset_step = jnp.where(own_layer, parity, parity * direction) * offset_size
    target_group = rotation_order[(rotation_place[home_group] + offset_step) % group_count]
    target_place = jnp.where(own_layer, jnp.bitwise_xor(home_place, 1), home_place)
    diagonal = own_layer & (slot_index == 0)
    target_group = jnp.where(diagonal, home_group, target_group)
    target_place = jnp.where(diagonal, home_place, target_place)
    columns = (target_group * OWN_BLOCKS + target_place).astype(jnp.int32)
    partner_row = target_group * ROW_BLOCKS + layer_ids * OWN_BLOCKS + target_place
    partner_flat = (partner_row * N_REP + home_class) * SLOTS + slot_index
    leading = (layer_ids > home_class) | own_layer & (slot_index > 0) & (home_place % 2 == 0)
    return (columns, partner_flat, leading, diagonal)


def draw_block_cols(key, part):
    return block_layout(key)[0]


def draw_block_vals(key, part):
    columns, partner_flat, leading, diagonal = block_layout(key)
    value_scale = (SLOTS * N_REP * BLOCK) ** (-0.5)
    self_flat = jnp.arange(BLOCKS * N_REP * SLOTS, dtype=jnp.int32).reshape(BLOCKS, N_REP, SLOTS)
    source_flat = jnp.where(leading | diagonal, self_flat, partner_flat).reshape(-1)
    value_key = jax.random.fold_in(key, 73)
    drawn = jax.vmap(lambda index: jax.random.normal(jax.random.fold_in(value_key, index), (BLOCK, BLOCK), jnp.float32))(source_flat)
    drawn = drawn.reshape(BLOCKS, N_REP, SLOTS, BLOCK, BLOCK) * value_scale
    turned = jnp.swapaxes(drawn, -1, -2)
    symmetric = (drawn + turned) * math.sqrt(0.5)
    result = jnp.where(diagonal[..., None, None], symmetric, jnp.where(leading[..., None, None], drawn, turned))
    return result.astype(jnp.bfloat16)


def level_of(own_key, shape, shards, low, top_value):
    loudness = 1.0
    for position, shards_of in shards:
        steps = jax.random.uniform(jax.random.fold_in(jax.random.fold_in(own_key, 6), position), (shards_of,), jnp.float32, low / len(shards), top_value / len(shards))
        loudness = loudness * jnp.repeat(jnp.exp(steps), shape[position] // shards_of).reshape((-1,) + (1,) * (len(shape) - 1 - position))
    return loudness


def gaussian(key, shape, scale, limit, split=(), kind=jnp.bfloat16):
    gain = level_of(key, shape, split, -0.22, 0.18) if split else 1.0
    entries = jax.random.normal(key, shape, jnp.float32) * scale * gain
    return jnp.minimum(jnp.maximum(entries, -limit), limit).astype(kind)


def setup_inputs(seed: int = 0) -> dict:
    key_list = jax.random.split(jax.random.key(seed), 6)
    return {
        "features": gaussian(key_list[0], (NODES, WIDTH), 1.0, 6.0, ((0, 32),)),
        "weight": gaussian(key_list[1], (WIDTH, WIDTH), WIDTH ** -0.5, 0.375),
        "block_cols": draw_block_cols(jax.random.fold_in(key_list[5], 71), 0),
        "block_vals": draw_block_vals(jax.random.fold_in(key_list[5], 71), 0),
        "out_grad": gaussian(key_list[4], (NODES, WIDTH), 1.0, 6.0, ((0, 8),)),
    }


def silu_parts(summed):
    sigmoid_vals = jax.nn.sigmoid(summed)
    return (summed * sigmoid_vals, sigmoid_vals * (1.0 + summed * (1.0 - sigmoid_vals)))

def column_blocks(block_cols):
    layer_ids = jnp.arange(N_REP, dtype=jnp.int32)[None, :, None]
    return block_cols // OWN_BLOCKS * ROW_BLOCKS + layer_ids * OWN_BLOCKS + block_cols % OWN_BLOCKS

def reference(features, weight, block_cols, block_vals, out_grad):
    mixed_rows = jnp.dot(features, weight, preferred_element_type=jnp.float32).astype(jnp.bfloat16)
    targets = column_blocks(block_cols)
    mixed_blocks = mixed_rows.reshape(BLOCKS, BLOCK, WIDTH)
    layer_range = jnp.arange(N_REP, dtype=jnp.int32)

    def forward_layer(running, layer_index):
        layer_vals = block_vals[:, layer_index].astype(jnp.float32)
        fetched = jnp.take(mixed_blocks, targets[:, layer_index], axis=0).astype(jnp.float32)
        return (running + jnp.einsum('bsij,bsjf->bif', layer_vals, fetched, precision=lax.Precision.HIGHEST), None)
    summed, _ = lax.scan(forward_layer, jnp.zeros((BLOCKS, BLOCK, WIDTH), jnp.float32), layer_range)
    summed = summed.reshape(NODES, WIDTH)
    values_all, slopes_all = silu_parts(summed)
    activations = values_all.astype(jnp.bfloat16)
    masked = (out_grad.astype(jnp.float32) * slopes_all).astype(jnp.bfloat16)
    grad_blocks = masked.reshape(BLOCKS, BLOCK, WIDTH).astype(jnp.float32)

    def backward_layer(running, layer_index):
        layer_vals = block_vals[:, layer_index].astype(jnp.float32)
        slot_terms = jnp.einsum('bsji,bjf->bsif', layer_vals, grad_blocks, precision=lax.Precision.HIGHEST)
        spread = jax.ops.segment_sum(slot_terms.reshape(BLOCKS * SLOTS, BLOCK, WIDTH), targets[:, layer_index].reshape(-1), num_segments=BLOCKS)
        return (running + spread, None)
    back_rows, _ = lax.scan(backward_layer, jnp.zeros((BLOCKS, BLOCK, WIDTH), jnp.float32), layer_range)
    back_rows = back_rows.reshape(NODES, WIDTH)
    weight_grad = jnp.dot(features.astype(jnp.float32).T, back_rows, precision=lax.Precision.HIGHEST) * (1.0 / math.sqrt(NODES))
    input_grad = jnp.dot(back_rows.astype(jnp.bfloat16), weight.T, preferred_element_type=jnp.float32).astype(jnp.bfloat16)
    return (activations, input_grad, weight_grad)
```

```python
import functools
import math

import jax
import jax.numpy as jnp
from jax import lax
from jax.experimental import pallas as pl
from jax.experimental.pallas import tpu as pltpu
from jax.sharding import PartitionSpec as P

F32 = jnp.float32
BF16 = jnp.bfloat16
HALF = 128
SCALE = 2.0**-21
VMEM = pl.BlockSpec(memory_space=pltpu.VMEM)
SMEM = pl.BlockSpec(memory_space=pltpu.SMEM)


def ring_order(n):
    return list(range(0, n, 2)) + list(range(n - 1, 0, -2))


def split_dot(left, right, dims):
    high = left.astype(BF16)
    low = (left - high.astype(F32)).astype(BF16)
    out = lax.dot_general(high, right, (dims, ((), ())), preferred_element_type=F32)
    return out + lax.dot_general(low, right, (dims, ((), ())), preferred_element_type=F32)


def gather_ring(chunks, n):
    order = ring_order(n)
    ahead = [(order[i], order[(i + 1) % n]) for i in range(n)]
    behind = [(b, a) for a, b in ahead]
    right, left = list(chunks), list(chunks)
    pieces = [[c] + [None] * (n - 1) for c in chunks]
    for step in range(1, n // 2 + 1):
        for k in range(len(chunks)):
            last = step == n // 2
            if not last or k % 2 == 0:
                right[k] = lax.ppermute(right[k], "rows", ahead)
                pieces[k][step] = right[k]
            if not last or k % 2 == 1:
                left[k] = lax.ppermute(left[k], "rows", behind)
                pieces[k][n - step] = left[k]
    return pieces


def blocks_kernel(n, own_blocks, block, where_ref, rep_ref, vals_ref, *refs):
    pieces, (send_far, send_near, keep_far, keep_near, pool) = refs[:n], refs[n:]
    rows = own_blocks * block
    for p in range(n):
        pool[p * rows : (p + 1) * rows, :] = pieces[p][...]
    me = rep_ref[0]
    for mask, out in ((3, send_far), (1, send_near), (2, keep_far), (0, keep_near)):
        base = lax.bitwise_xor(me, mask) * own_blocks
        for j in range(own_blocks):
            total = None
            for s in range(2):
                item = (base + j) * 2 + s
                start = pl.multiple_of(where_ref[item] * block, block)
                term = jnp.dot(vals_ref[item], pool[pl.ds(start, block), :], preferred_element_type=F32)
                total = term if total is None else total + term
            out[j * block : (j + 1) * block, :] = total.astype(out.dtype)


def apply_blocks(where, rep, vals, pieces, own_blocks):
    n, block = len(pieces), vals.shape[-1]
    rows, width = pieces[0].shape
    shapes = [jax.ShapeDtypeStruct((rows, width), t) for t in (BF16, BF16, F32, F32)]
    size = vals.size * 2 + 2 * n * rows * width * 2 + rows * width * 12
    return pl.pallas_call(
        functools.partial(blocks_kernel, n, own_blocks, block),
        out_shape=shapes,
        in_specs=[SMEM, SMEM, VMEM] + [VMEM] * n,
        out_specs=[VMEM] * 4,
        scratch_shapes=[pltpu.VMEM((n * rows, width), BF16)],
        compiler_params=pltpu.CompilerParams(vmem_limit_bytes=size + (8 << 20)),
        cost_estimate=pl.CostEstimate(
            flops=2 * vals.size * width, bytes_accessed=size, transcendentals=0
        ),
        name="apply_blocks",
    )(where, rep, vals, *pieces)


def reduce_rep(parts):
    send_far, send_near, keep_far, keep_near = parts
    swap = [(i, i ^ 1) for i in range(4)]
    cross = [(i, i ^ 2) for i in range(4)]
    got_far = lax.ppermute(send_far, "rep", swap)
    got_near = lax.ppermute(send_near, "rep", swap)
    crossing = (keep_far + got_far.astype(F32)).astype(BF16)
    return keep_near, got_near, lax.ppermute(crossing, "rep", cross)


def joined(refs):
    halves = []
    for h in range(len(refs) // 3):
        near, got, cross = refs[3 * h : 3 * h + 3]
        halves.append(near[...] + got[...].astype(F32) + cross[...].astype(F32))
    return jnp.concatenate(halves, axis=1)


def middle_kernel(weight_ref, grad_ref, *refs):
    sums, (act_ref, held_ref, *masked_refs) = refs[:6], refs[6:]
    held = joined(sums)
    held_ref[...] = held
    summed = split_dot(held, weight_ref[...], ((1,), (0,))) * (1.0 / SCALE)
    gate = jax.nn.sigmoid(summed)
    act_ref[...] = (summed * gate).astype(BF16)
    slope = gate * (1.0 + summed * (1.0 - gate))
    masked = (grad_ref[...].astype(F32) * slope).astype(BF16)
    for h, ref in enumerate(masked_refs):
        ref[...] = masked[:, h * HALF : (h + 1) * HALF]


def middle(weight, grad, sums):
    rows, width = grad.shape
    shapes = [jax.ShapeDtypeStruct((rows, width), BF16), jax.ShapeDtypeStruct((rows, width), F32)]
    shapes += [jax.ShapeDtypeStruct((rows, HALF), BF16)] * (width // HALF)
    return pl.pallas_call(
        middle_kernel,
        out_shape=shapes,
        in_specs=[VMEM] * 8,
        out_specs=[VMEM] * len(shapes),
        compiler_params=pltpu.CompilerParams(vmem_limit_bytes=24 << 20),
        cost_estimate=pl.CostEstimate(
            flops=4 * rows * width * width, bytes_accessed=rows * width * 18, transcendentals=rows * width
        ),
        name="middle",
    )(weight, grad, *sums)


def last_kernel(weight_ref, *refs):
    back = joined(refs[:6])
    refs[6][...] = split_dot(back, weight_ref[...], ((1,), (1,))).astype(BF16)


def last(weight, sums):
    rows, width = sums[0].shape[0], weight.shape[0]
    return pl.pallas_call(
        last_kernel,
        out_shape=jax.ShapeDtypeStruct((rows, width), BF16),
        in_specs=[VMEM] * 7,
        out_specs=VMEM,
        compiler_params=pltpu.CompilerParams(vmem_limit_bytes=24 << 20),
        cost_estimate=pl.CostEstimate(
            flops=4 * rows * width * width, bytes_accessed=rows * width * 14, transcendentals=0
        ),
        name="last",
    )(weight, *sums)


def sum_everywhere(value, n):
    layer = lax.axis_index("rep")
    for bit in (0, 1):
        half = value.shape[0] // 2
        mine = lax.shift_right_logical(layer, bit) & 1
        pair = [(i, i ^ (1 << bit)) for i in range(4)]
        got = lax.ppermute(lax.dynamic_slice_in_dim(value, (1 - mine) * half, half, 0), "rep", pair)
        value = lax.dynamic_slice_in_dim(value, mine * half, half, 0) + got
    step = 1
    while step < n:
        value = value + lax.ppermute(value, "rows", [(i, i ^ step) for i in range(n)])
        step *= 2
    for bit in (1, 0):
        mine = lax.shift_right_logical(layer, bit) & 1
        other = lax.ppermute(value, "rep", [(i, i ^ (1 << bit)) for i in range(4)])
        value = jnp.where(
            mine == 0, jnp.concatenate([value, other], 0), jnp.concatenate([other, value], 0)
        )
    return value


def on_device(n, features, weight, block_cols, block_vals, out_grad):
    own_rows, width = features.shape
    block = block_vals.shape[-1]
    own_blocks = own_rows // block
    me, layer = lax.axis_index("rows"), lax.axis_index("rep")
    order = ring_order(n)
    place = [order.index(i) for i in range(n)]
    place = jnp.array(place, jnp.int32)
    cols = block_cols.reshape(-1)
    owners = cols // own_blocks
    owner_place = jnp.sum(
        jnp.where(owners[:, None] == jnp.arange(n, dtype=jnp.int32)[None, :], place[None, :], 0), axis=1
    )
    back_steps = (place[me] - owner_place + n) % n
    where = back_steps * own_blocks + cols % own_blocks
    rep = layer.astype(jnp.int32).reshape(1)
    vals = block_vals.reshape(-1, block, block)
    halves = width // HALF
    scaled = features * jnp.asarray(SCALE, BF16)

    def spread(chunks):
        sums = []
        for pieces in gather_ring(chunks, n):
            sums += reduce_rep(apply_blocks(where, rep, vals, pieces, own_blocks))
        return sums

    grad = lax.dynamic_slice_in_dim(out_grad, layer * own_rows, own_rows, 0)
    sums = spread([scaled[:, h * HALF : (h + 1) * HALF] for h in range(halves)])
    activated, held, *masked = middle(weight, grad, sums)
    local = jnp.concatenate([split_dot(held, m, ((0,), (0,))) for m in masked], axis=1)
    node_total = own_rows * n * 4
    weight_grad = sum_everywhere(local, n) * (1.0 / (SCALE * math.sqrt(node_total)))
    input_grad = last(weight, spread(masked))
    return activated, input_grad, weight_grad


def solution(mesh):
    placed = (
        P(("rows", "rep"), None),
        P(),
        P("rows", "rep", None),
        P("rows", "rep", None, None, None),
        P("rows", None),
    )
    return jax.shard_map(
        functools.partial(on_device, mesh.shape["rows"]),
        mesh=mesh,
        in_specs=placed,
        out_specs=(P(("rows", "rep"), None), P(("rows", "rep"), None), P()),
        check_vma=False,
    )
```

```python
import functools
import math

import jax
import jax.numpy as jnp
from jax import lax
from jax.experimental import pallas as pl
from jax.experimental.pallas import tpu as pltpu
from jax.sharding import PartitionSpec as P

F32 = jnp.float32
BF16 = jnp.bfloat16
HALF = 128
SCALE = 2.0**-21
VMEM = pl.BlockSpec(memory_space=pltpu.VMEM)
SMEM = pl.BlockSpec(memory_space=pltpu.SMEM)


def ring_order(n):
    return list(range(0, n, 2)) + list(range(n - 1, 0, -2))


def ring_place(i, n):
    return jnp.where(i % 2 == 0, i // 2, n - 1 - i // 2)


def split_dot(left, right, dims):
    high = left.astype(BF16)
    low = (left - high.astype(F32)).astype(BF16)
    out = lax.dot_general(high, right, (dims, ((), ())), preferred_element_type=F32)
    return out + lax.dot_general(low, right, (dims, ((), ())), preferred_element_type=F32)


def tie(arrays, other):
    return lax.optimization_barrier((arrays, other))[0]


def gather_ring(chunks, n, beside=None):
    order = ring_order(n)
    ahead = [(order[i], order[(i + 1) % n]) for i in range(n)]
    behind = [(b, a) for a, b in ahead]
    right, left = list(chunks), list(chunks)
    pieces = [[c] + [None] * (n - 1) for c in chunks]
    for step in range(1, n // 2 + 1):
        for k in range(len(chunks)):
            last = step == n // 2
            if beside and (step, k) in beside:
                right[k], left[k] = tie((right[k], left[k]), beside[step, k](before))
            before = right[k]
            if not last or k % 2 == 0:
                right[k] = lax.ppermute(right[k], "rows", ahead)
                pieces[k][step] = right[k]
            if not last or k % 2 == 1:
                left[k] = lax.ppermute(left[k], "rows", behind)
                pieces[k][n - step] = left[k]
    return pieces


def blocks_kernel(n, own_blocks, block, scale, where_ref, rep_ref, vals_ref, *refs):
    pieces, (send, keep_far, keep_near, pool) = refs[:n], refs[n:]
    rows = own_blocks * block
    for p in range(n):
        piece = pieces[p][...]
        pool[p * rows : (p + 1) * rows, :] = piece if scale is None else piece * jnp.asarray(scale, BF16)
    me = rep_ref[0]
    for mask, out, first in ((3, send, 0), (1, send, own_blocks), (2, keep_far, 0), (0, keep_near, 0)):
        base = lax.bitwise_xor(me, mask) * own_blocks
        for j in range(own_blocks):
            total = None
            for s in range(2):
                item = (base + j) * 2 + s
                start = pl.multiple_of(where_ref[item] * block, block)
                term = jnp.dot(vals_ref[item], pool[pl.ds(start, block), :], preferred_element_type=F32)
                total = term if total is None else total + term
            out[(first + j) * block : (first + j + 1) * block, :] = total.astype(out.dtype)


def apply_blocks(where, rep, vals, pieces, own_blocks, scale):
    n, block = len(pieces), vals.shape[-1]
    rows, width = pieces[0].shape
    shapes = [jax.ShapeDtypeStruct((2 * rows, width), BF16)]
    shapes += [jax.ShapeDtypeStruct((rows, width), F32)] * 2
    size = vals.size * 2 + 2 * n * rows * width * 2 + rows * width * 12
    return pl.pallas_call(
        functools.partial(blocks_kernel, n, own_blocks, block, scale),
        out_shape=shapes,
        in_specs=[SMEM, SMEM, VMEM] + [VMEM] * n,
        out_specs=[VMEM] * 3,
        scratch_shapes=[pltpu.VMEM((n * rows, width), BF16)],
        compiler_params=pltpu.CompilerParams(vmem_limit_bytes=size + (8 << 20)),
        cost_estimate=pl.CostEstimate(
            flops=2 * vals.size * width, bytes_accessed=size, transcendentals=0
        ),
        name="apply_blocks",
    )(where, rep, vals, *pieces)


def reduce_rep(parts):
    send, keep_far, keep_near = parts
    got = lax.ppermute(send, "rep", [(i, i ^ 1) for i in range(4)])
    crossing = (keep_far + got[: keep_far.shape[0]].astype(F32)).astype(BF16)
    return keep_near, got, lax.ppermute(crossing, "rep", [(i, i ^ 2) for i in range(4)]), crossing


def joined(refs):
    halves = []
    for h in range(len(refs) // 3):
        near, got, cross = refs[3 * h : 3 * h + 3]
        rows = near.shape[0]
        halves.append(near[...] + got[rows:, :].astype(F32) + cross[...].astype(F32))
    return jnp.concatenate(halves, axis=1)


def middle_kernel(rep_ref, weight_ref, grad_ref, *refs):
    sums, (act_ref, high_ref, low_ref, *masked_refs, grad, sem) = refs[:6], refs[6:]
    rows = act_ref.shape[0]
    start = pl.multiple_of(rep_ref[0] * rows, rows)
    copy = pltpu.make_async_copy(grad_ref.at[pl.ds(start, rows), :], grad, sem)
    copy.start()
    held = joined(sums)
    high = held.astype(BF16)
    low = (held - high.astype(F32)).astype(BF16)
    high_ref[...] = high
    low_ref[...] = low
    weight = weight_ref[...]
    summed = jnp.dot(high, weight, preferred_element_type=F32)
    summed = (summed + jnp.dot(low, weight, preferred_element_type=F32)) * (1.0 / SCALE)
    gate = jax.nn.sigmoid(summed)
    act_ref[...] = (summed * gate).astype(BF16)
    slope = gate * (1.0 + summed * (1.0 - gate))
    copy.wait()
    masked = (grad[...].astype(F32) * slope).astype(BF16)
    for h, ref in enumerate(masked_refs):
        ref[...] = masked[:, h * HALF : (h + 1) * HALF]


def middle(rep, weight, grad, sums):
    rows, width = sums[0].shape[0], grad.shape[1]
    shapes = [jax.ShapeDtypeStruct((rows, width), BF16)] * 3
    shapes += [jax.ShapeDtypeStruct((rows, HALF), BF16)] * (width // HALF)
    return pl.pallas_call(
        middle_kernel,
        out_shape=shapes,
        in_specs=[SMEM, VMEM, pl.BlockSpec(memory_space=pl.ANY)] + [VMEM] * 6,
        out_specs=[VMEM] * len(shapes),
        scratch_shapes=[pltpu.VMEM((rows, width), BF16), pltpu.SemaphoreType.DMA],
        compiler_params=pltpu.CompilerParams(vmem_limit_bytes=16 << 20),
        cost_estimate=pl.CostEstimate(
            flops=4 * rows * width * width, bytes_accessed=rows * width * 18, transcendentals=rows * width
        ),
        name="middle",
    )(rep, weight, grad, *sums)


def last_kernel(weight_ref, *refs):
    back = joined(refs[:6])
    refs[6][...] = split_dot(back, weight_ref[...], ((1,), (1,))).astype(BF16)


def last(weight, sums):
    rows, width = sums[0].shape[0], weight.shape[0]
    return pl.pallas_call(
        last_kernel,
        out_shape=jax.ShapeDtypeStruct((rows, width), BF16),
        in_specs=[VMEM] * 7,
        out_specs=VMEM,
        compiler_params=pltpu.CompilerParams(vmem_limit_bytes=24 << 20),
        cost_estimate=pl.CostEstimate(
            flops=4 * rows * width * width, bytes_accessed=rows * width * 14, transcendentals=0
        ),
        name="last",
    )(weight, *sums)


def local_kernel(rep_ref, high_ref, low_ref, *refs):
    masked, outs = refs[:2], refs[2:6]
    total = refs[6]
    for h, ref in enumerate(masked):
        part = None
        for held in (high_ref, low_ref):
            term = lax.dot_general(held[...], ref[...], (((0,), (0,)), ((), ())), preferred_element_type=F32)
            part = term if part is None else part + term
        total[:, h * HALF : (h + 1) * HALF] = part
    rows = outs[0].shape[0]
    for mask, out in enumerate(outs):
        start = pl.multiple_of(lax.bitwise_xor(rep_ref[0], mask) * rows, rows)
        out[...] = total[pl.ds(start, rows), :]


def local_grad(rep, high, low, masked):
    rows, width = high.shape
    return pl.pallas_call(
        local_kernel,
        out_shape=[jax.ShapeDtypeStruct((width // 4, width), F32)] * 4,
        in_specs=[SMEM] + [VMEM] * 4,
        out_specs=[VMEM] * 4,
        scratch_shapes=[pltpu.VMEM((width, width), F32)],
        compiler_params=pltpu.CompilerParams(vmem_limit_bytes=16 << 20),
        cost_estimate=pl.CostEstimate(
            flops=4 * rows * width * width, bytes_accessed=rows * width * 6, transcendentals=0
        ),
        name="local_grad",
    )(rep, high, low, *masked)


def whole_kernel(scale, rep_ref, *refs):
    rows = refs[0].shape[0]
    for mask in range(4):
        start = pl.multiple_of(lax.bitwise_xor(rep_ref[0], mask) * rows, rows)
        refs[4][pl.ds(start, rows), :] = refs[mask][...] * scale


def whole_grad(rep, quarters, scale):
    rows, width = quarters[0].shape
    return pl.pallas_call(
        functools.partial(whole_kernel, scale),
        out_shape=jax.ShapeDtypeStruct((4 * rows, width), F32),
        in_specs=[SMEM] + [VMEM] * 4,
        out_specs=VMEM,
        compiler_params=pltpu.CompilerParams(vmem_limit_bytes=4 << 20),
        name="whole_grad",
    )(rep, *quarters)


class GradientSum:
    def __init__(self, rep, high, low, masked, n, scale):
        self.rep, self.local, self.n, self.scale = rep, (high, low, masked), n, scale
        self.pairs = [[(i, i ^ mask) for i in range(4)] for mask in range(4)]

    def start(self, after):
        high, low, masked = tie(self.local, after)
        self.quarters = local_grad(self.rep, high, low, masked)
        return self.quarters

    def over_rep(self, after):
        value = self.quarters[0]
        for mask in (1, 2, 3):
            value = value + lax.ppermute(self.quarters[mask], "rep", self.pairs[mask])
        self.value = value
        return value

    def over_rows(self, strides):
        value = self.value
        pairs = [[(i, i ^ step) for i in range(self.n)] for step in range(self.n)]
        if len(strides) == 2:
            low, high = strides
            near = value + lax.ppermute(value, "rows", pairs[low])
            far = [lax.ppermute(value, "rows", pairs[step]) for step in (high, high + low)]
            self.value = near + (far[0] + far[1])
        else:
            for step in strides:
                value = value + lax.ppermute(value, "rows", pairs[step])
            self.value = value
        return self.value

    def finish(self, after):
        self.value = tie(self.value, after)
        others = [lax.ppermute(self.value, "rep", self.pairs[mask]) for mask in (1, 2, 3)]
        return whole_grad(self.rep, [self.value, *others], self.scale)


def on_device(n, features, weight, block_cols, block_vals, out_grad):
    own_rows, width = features.shape
    block = block_vals.shape[-1]
    own_blocks = own_rows // block
    me, layer = lax.axis_index("rows"), lax.axis_index("rep")
    vals = block_vals.reshape(-1, block, block)
    chunks = [features[:, h * HALF : (h + 1) * HALF] for h in range(width // HALF)]
    ready = {}

    def prepared(after):
        my, rep, cols = tie((me.astype(jnp.int32), layer.astype(jnp.int32).reshape(1), block_cols), after)
        cols = cols.reshape(-1)
        back_steps = (ring_place(my, n) - ring_place(cols // own_blocks, n) + n) % n
        ready["rep"], ready["where"] = rep, back_steps * own_blocks + cols % own_blocks
        return ready["rep"], ready["where"]

    sums = []
    for pieces in gather_ring(chunks, n, {(2, 1): prepared}):
        parts = apply_blocks(ready["where"], ready["rep"], vals, pieces, own_blocks, SCALE)
        sums += reduce_rep(parts)[:3]
    rep = ready["rep"]
    activated, high, low, *masked = middle(rep, weight, out_grad, sums)

    node_total = own_rows * n * 4
    grad = GradientSum(rep, high, low, masked, n, 1.0 / (SCALE * math.sqrt(node_total)))
    beside = {(2, 0): grad.start, (3, 0): grad.over_rep, (4, 0): lambda _: grad.over_rows([1])}
    gathered = gather_ring(masked, n, beside)
    gathered[1] = tie(gathered[1], grad.over_rows([1 << i for i in range(1, n.bit_length() - 1)]))
    sums = []
    for pieces in gathered:
        parts = apply_blocks(ready["where"], rep, vals, pieces, own_blocks, None)
        *parts, crossing = reduce_rep(parts)
        sums += parts
    weight_grad = grad.finish(crossing)
    input_grad = last(weight, sums)
    return activated, input_grad, weight_grad


def solution(mesh):
    placed = (
        P(("rows", "rep"), None),
        P(),
        P("rows", "rep", None),
        P("rows", "rep", None, None, None),
        P("rows", None),
    )
    return jax.shard_map(
        functools.partial(on_device, mesh.shape["rows"]),
        mesh=mesh,
        in_specs=placed,
        out_specs=(P(("rows", "rep"), None), P(("rows", "rep"), None), P()),
        check_vma=False,
    )
```

```python
import functools
import math

import jax
import jax.numpy as jnp
from jax import lax
from jax.experimental import pallas as pl
from jax.experimental.pallas import tpu as pltpu
from jax.sharding import PartitionSpec as P

F32 = jnp.float32
BF16 = jnp.bfloat16
HALF = 128
SCALE = 2.0**-21
VMEM = pl.BlockSpec(memory_space=pltpu.VMEM)
SMEM = pl.BlockSpec(memory_space=pltpu.SMEM)


def ring_order(n):
    return list(range(0, n, 2)) + list(range(n - 1, 0, -2))


def ring_place(i, n):
    return jnp.where(i % 2 == 0, i // 2, n - 1 - i // 2)


def split_dot(left, right, dims):
    high = left.astype(BF16)
    low = (left - high.astype(F32)).astype(BF16)
    out = lax.dot_general(high, right, (dims, ((), ())), preferred_element_type=F32)
    return out + lax.dot_general(low, right, (dims, ((), ())), preferred_element_type=F32)


def tie(arrays, other):
    return lax.optimization_barrier((arrays, other))[0]


def ring_ways(n):
    order = ring_order(n)
    ahead = [(order[i], order[(i + 1) % n]) for i in range(n)]
    return ahead, [(b, a) for a, b in ahead]


def gather_kernel(n, own_blocks, block, scale, where_ref, rep_ref, vals_ref, *refs):
    pieces, (send, keep_far, keep_near, pool) = refs[: n + 1], refs[n + 1 :]
    rows, half = own_blocks * block, n // 2
    starts = [p * rows for p in range(half + 1)] + [half * rows + rows // 2]
    starts += [p * rows for p in range(half + 1, n)]
    for start, ref in zip(starts, pieces):
        piece = ref[...]
        pool[start : start + piece.shape[0], :] = piece if scale is None else piece * jnp.asarray(scale, BF16)
    me = rep_ref[0]
    for mask, out, first in ((3, send, 0), (1, send, own_blocks), (2, keep_far, 0), (0, keep_near, 0)):
        base = lax.bitwise_xor(me, mask) * own_blocks
        for j in range(own_blocks):
            total = None
            for s in range(2):
                item = (base + j) * 2 + s
                start = pl.multiple_of(where_ref[item] * block, block)
                term = jnp.dot(vals_ref[item], pool[pl.ds(start, block), :], preferred_element_type=F32)
                total = term if total is None else total + term
            out[(first + j) * block : (first + j + 1) * block, :] = total.astype(out.dtype)


def gather_blocks(where, rep, vals, pieces, n, own_blocks, scale):
    block = vals.shape[-1]
    rows, width = pieces[0].shape
    shapes = [jax.ShapeDtypeStruct((2 * rows, width), BF16)]
    shapes += [jax.ShapeDtypeStruct((rows, width), F32)] * 2
    size = vals.size * 2 + 2 * n * rows * width * 2 + rows * width * 12
    return pl.pallas_call(
        functools.partial(gather_kernel, n, own_blocks, block, scale),
        out_shape=shapes,
        in_specs=[SMEM, SMEM, VMEM] + [VMEM] * (n + 1),
        out_specs=[VMEM] * 3,
        scratch_shapes=[pltpu.VMEM((n * rows, width), BF16)],
        compiler_params=pltpu.CompilerParams(vmem_limit_bytes=size + (8 << 20)),
        cost_estimate=pl.CostEstimate(
            flops=2 * vals.size * width, bytes_accessed=size, transcendentals=0
        ),
        name="gather_blocks",
    )(where, rep, vals, *pieces)


def scatter_kernel(own_blocks, block, scale, where_ref, rep_ref, vals_ref, *refs):
    sources, (own_ref, out_ref) = refs[:4], refs[4:]
    rows = own_blocks * block
    out_ref[...] = jnp.zeros_like(out_ref)
    me = rep_ref[0]
    for mask in range(4):
        base = lax.bitwise_xor(me, mask) * own_blocks
        for j in range(own_blocks):
            source = sources[mask][j * block : (j + 1) * block, :]
            if scale is not None:
                source = source * jnp.asarray(scale, BF16)
            for s in range(2):
                item = (base + j) * 2 + s
                start = pl.multiple_of(where_ref[item] * block, block)
                term = lax.dot_general(vals_ref[item], source, (((0,), (0,)), ((), ())), preferred_element_type=F32)
                out_ref[pl.ds(start, block), :] += term
    own_ref[...] = out_ref[:rows, :]


def scatter_blocks(where, rep, vals, sources, n, own_blocks, scale):
    block = vals.shape[-1]
    rows, width = sources[0].shape
    size = vals.size * 2 + 4 * rows * width * 2 + (n + 1) * rows * width * 4
    return pl.pallas_call(
        functools.partial(scatter_kernel, own_blocks, block, scale),
        out_shape=[jax.ShapeDtypeStruct((rows, width), F32), jax.ShapeDtypeStruct((n * rows, width), F32)],
        in_specs=[SMEM, SMEM, VMEM] + [VMEM] * 4,
        out_specs=[VMEM] * 2,
        compiler_params=pltpu.CompilerParams(vmem_limit_bytes=size + (4 << 20)),
        cost_estimate=pl.CostEstimate(
            flops=2 * vals.size * width, bytes_accessed=size, transcendentals=0
        ),
        name="scatter_blocks",
    )(where, rep, vals, *sources)


def near_kernel(vals_ref, out_ref):
    out_ref[...] = vals_ref[0, :8, :]


def brought_near(vals):
    return pl.pallas_call(
        near_kernel,
        out_shape=jax.ShapeDtypeStruct((8, vals.shape[-1]), vals.dtype),
        in_specs=[VMEM],
        out_specs=VMEM,
        compiler_params=pltpu.CompilerParams(vmem_limit_bytes=4 << 20),
        name="brought_near",
    )(vals)


def add_terms(pair, terms, sent):
    right, left = (array.astype(F32) for array in pair)
    mid = terms[0].shape[0] // 2
    if right.shape[0] == mid:
        right = jnp.concatenate([terms[0][:mid] + right, terms[0][mid:]], 0)
        left = jnp.concatenate([terms[1][:mid], terms[1][mid:] + left], 0)
    else:
        right, left = terms[0] + right, terms[1] + left
    return right.astype(sent), left.astype(sent)


def spread(first, second, n, own_blocks, numbers, vals, scale, hooks):
    ahead, behind = ring_ways(n)
    rows, half = first.shape[0], n // 2
    mid = rows // 2
    sent = BF16 if n <= 8 else F32
    pairs = [[(i, i ^ mask) for i in range(4)] for mask in range(4)]
    hook = lambda name, after: hooks[name](after) if name in hooks else ()
    step = lambda pair: (lax.ppermute(pair[0], "rows", ahead), lax.ppermute(pair[1], "rows", behind))

    across = lax.ppermute(second, "rep", pairs[2])
    beside = lax.ppermute(tie(second, hook("beside", ())), "rep", pairs[1])
    gathered = step((first, first))
    pieces = [first] + [None] * n
    pieces[1], pieces[n] = gathered
    moving = None
    for hop in range(2, half + 1):
        if hop == 2:
            gathered = tie(gathered, (across, hook("gather 2", across)))
            far = lax.ppermute(across, "rep", pairs[1])
        else:
            gathered = tie(gathered, (moving, hook("gather %d" % hop, moving)))
        if hop == half:
            gathered = gathered[0][:mid], gathered[1][mid:]
        behind_it = gathered
        gathered = step(gathered)
        pieces[hop], pieces[n + 1 - hop] = gathered
        if hop == 2:
            where, rep = numbers()
            sources = tie([second, beside, across, far], behind_it)
            own, partial = scatter_blocks(where, rep, vals, sources, n, own_blocks, scale)
            term = lambda distance: partial[distance * rows : (distance + 1) * rows]
            moving = term(half)[:mid].astype(sent), term(half)[mid:].astype(sent)
        else:
            moving = tie(add_terms(step(moving), (term(half + hop - 2), term(half - hop + 2)), sent), behind_it)
    pieces = tie(pieces, (moving, hook("blocks", moving)))
    *summed, crossing = reduce_rep(gather_blocks(where, rep, vals, pieces, n, own_blocks, scale))
    moving = add_terms(step(moving), (term(n - 1), term(1)), sent)
    moving = tie(moving, (crossing, hook("last", crossing)))
    right, left = step(moving)
    return [*summed, own, right, left], moving


def reduce_rep(parts):
    send, keep_far, keep_near = parts
    got = lax.ppermute(send, "rep", [(i, i ^ 1) for i in range(4)])
    crossing = (keep_far + got[: keep_far.shape[0]].astype(F32)).astype(BF16)
    return keep_near, got, lax.ppermute(crossing, "rep", [(i, i ^ 2) for i in range(4)]), crossing


def joined(refs):
    near, got, cross, own, right, left = refs
    rows = near.shape[0]
    first = near[...] + got[rows:, :].astype(F32) + cross[...].astype(F32)
    second = own[...] + (right[...].astype(F32) + left[...].astype(F32))
    return jnp.concatenate([first, second], axis=1)


def middle_kernel(rep_ref, weight_ref, grad_ref, *refs):
    sums, (act_ref, high_ref, low_ref, *masked_refs, grad, sem) = refs[:6], refs[6:]
    rows = act_ref.shape[0]
    start = pl.multiple_of(rep_ref[0] * rows, rows)
    copy = pltpu.make_async_copy(grad_ref.at[pl.ds(start, rows), :], grad, sem)
    copy.start()
    held = joined(sums)
    high = held.astype(BF16)
    low = (held - high.astype(F32)).astype(BF16)
    high_ref[...] = high
    low_ref[...] = low
    weight = weight_ref[...]
    summed = jnp.dot(high, weight, preferred_element_type=F32)
    summed = (summed + jnp.dot(low, weight, preferred_element_type=F32)) * (1.0 / SCALE)
    gate = jax.nn.sigmoid(summed)
    act_ref[...] = (summed * gate).astype(BF16)
    slope = gate * (1.0 + summed * (1.0 - gate))
    copy.wait()
    masked = (grad[...].astype(F32) * slope).astype(BF16)
    for h, ref in enumerate(masked_refs):
        ref[...] = masked[:, h * HALF : (h + 1) * HALF]


def middle(rep, weight, grad, sums):
    rows, width = sums[0].shape[0], grad.shape[1]
    shapes = [jax.ShapeDtypeStruct((rows, width), BF16)] * 3
    shapes += [jax.ShapeDtypeStruct((rows, HALF), BF16)] * (width // HALF)
    return pl.pallas_call(
        middle_kernel,
        out_shape=shapes,
        in_specs=[SMEM, VMEM, pl.BlockSpec(memory_space=pl.ANY)] + [VMEM] * 6,
        out_specs=[VMEM] * len(shapes),
        scratch_shapes=[pltpu.VMEM((rows, width), BF16), pltpu.SemaphoreType.DMA],
        compiler_params=pltpu.CompilerParams(vmem_limit_bytes=16 << 20),
        cost_estimate=pl.CostEstimate(
            flops=4 * rows * width * width, bytes_accessed=rows * width * 18, transcendentals=rows * width
        ),
        name="middle",
    )(rep, weight, grad, *sums)


def last_kernel(weight_ref, *refs):
    back = joined(refs[:6])
    refs[6][...] = split_dot(back, weight_ref[...], ((1,), (1,))).astype(BF16)


def last(weight, sums):
    rows, width = sums[0].shape[0], weight.shape[0]
    return pl.pallas_call(
        last_kernel,
        out_shape=jax.ShapeDtypeStruct((rows, width), BF16),
        in_specs=[VMEM] * 7,
        out_specs=VMEM,
        compiler_params=pltpu.CompilerParams(vmem_limit_bytes=24 << 20),
        cost_estimate=pl.CostEstimate(
            flops=4 * rows * width * width, bytes_accessed=rows * width * 14, transcendentals=0
        ),
        name="last",
    )(weight, *sums)


def local_kernel(rep_ref, high_ref, low_ref, *refs):
    masked, outs = refs[:2], refs[2:6]
    total = refs[6]
    for h, ref in enumerate(masked):
        part = None
        for held in (high_ref, low_ref):
            term = lax.dot_general(held[...], ref[...], (((0,), (0,)), ((), ())), preferred_element_type=F32)
            part = term if part is None else part + term
        total[:, h * HALF : (h + 1) * HALF] = part
    rows = outs[0].shape[0]
    for mask, out in enumerate(outs):
        start = pl.multiple_of(lax.bitwise_xor(rep_ref[0], mask) * rows, rows)
        out[...] = total[pl.ds(start, rows), :]


def local_grad(rep, high, low, masked):
    rows, width = high.shape
    return pl.pallas_call(
        local_kernel,
        out_shape=[jax.ShapeDtypeStruct((width // 4, width), F32)] * 4,
        in_specs=[SMEM] + [VMEM] * 4,
        out_specs=[VMEM] * 4,
        scratch_shapes=[pltpu.VMEM((width, width), F32)],
        compiler_params=pltpu.CompilerParams(vmem_limit_bytes=16 << 20),
        cost_estimate=pl.CostEstimate(
            flops=4 * rows * width * width, bytes_accessed=rows * width * 6, transcendentals=0
        ),
        name="local_grad",
    )(rep, high, low, *masked)


def whole_kernel(scale, rep_ref, *refs):
    rows = refs[0].shape[0]
    for mask in range(4):
        start = pl.multiple_of(lax.bitwise_xor(rep_ref[0], mask) * rows, rows)
        refs[4][pl.ds(start, rows), :] = refs[mask][...] * scale


def whole_grad(rep, quarters, scale):
    rows, width = quarters[0].shape
    return pl.pallas_call(
        functools.partial(whole_kernel, scale),
        out_shape=jax.ShapeDtypeStruct((4 * rows, width), F32),
        in_specs=[SMEM] + [VMEM] * 4,
        out_specs=VMEM,
        compiler_params=pltpu.CompilerParams(vmem_limit_bytes=4 << 20),
        name="whole_grad",
    )(rep, *quarters)


class GradientSum:
    def __init__(self, rep, high, low, masked, n, scale):
        self.rep, self.local, self.n, self.scale = rep, (high, low, masked), n, scale
        self.pairs = [[(i, i ^ mask) for i in range(4)] for mask in range(4)]

    def start(self, after):
        high, low, masked = tie(self.local, after)
        self.quarters = local_grad(self.rep, high, low, masked)
        return self.quarters

    def over_rep(self, after):
        value = self.quarters[0]
        for mask in (1, 2, 3):
            value = value + lax.ppermute(self.quarters[mask], "rep", self.pairs[mask])
        self.value = value
        return value

    def over_rows(self, strides):
        value = self.value
        pairs = [[(i, i ^ step) for i in range(self.n)] for step in range(self.n)]
        if len(strides) == 2:
            low, high = strides
            near = value + lax.ppermute(value, "rows", pairs[low])
            far = [lax.ppermute(value, "rows", pairs[step]) for step in (high, high + low)]
            self.value = near + (far[0] + far[1])
        else:
            for step in strides:
                value = value + lax.ppermute(value, "rows", pairs[step])
            self.value = value
        return self.value

    def finish(self, after):
        self.value = tie(self.value, after)
        others = [lax.ppermute(self.value, "rep", self.pairs[mask]) for mask in (1, 2, 3)]
        return whole_grad(self.rep, [self.value, *others], self.scale)


def on_device(n, features, weight, block_cols, block_vals, out_grad):
    own_rows, width = features.shape
    block = block_vals.shape[-1]
    own_blocks = own_rows // block
    me, layer = lax.axis_index("rows"), lax.axis_index("rep")
    vals = block_vals.reshape(-1, block, block)
    chunks = [features[:, h * HALF : (h + 1) * HALF] for h in range(width // HALF)]
    ready = {}

    def prepared(after):
        my, rep, cols = tie((me.astype(jnp.int32), layer.astype(jnp.int32).reshape(1), block_cols), after)
        cols = cols.reshape(-1)
        back_steps = (ring_place(my, n) - ring_place(cols // own_blocks, n) + n) % n
        ready["rep"], ready["where"] = rep, back_steps * own_blocks + cols % own_blocks
        return ready["rep"], ready["where"], brought_near(vals)

    numbers = lambda: (ready["where"], ready["rep"])
    sums, _ = spread(*chunks, n, own_blocks, numbers, vals, SCALE, {"beside": prepared})
    rep = ready["rep"]
    activated, high, low, *masked = middle(rep, weight, out_grad, sums)

    node_total = own_rows * n * 4
    grad = GradientSum(rep, high, low, masked, n, 1.0 / (SCALE * math.sqrt(node_total)))
    hooks = {"gather 2": grad.start, "gather 3": grad.over_rep, "gather 4": lambda _: grad.over_rows([1])}
    hooks["last"] = lambda _: grad.over_rows([1 << i for i in range(1, n.bit_length() - 1)])
    sums, moving = spread(*masked, n, own_blocks, numbers, vals, None, hooks)
    weight_grad = grad.finish(moving)
    input_grad = last(weight, sums)
    return activated, input_grad, weight_grad


def solution(mesh):
    placed = (
        P(("rows", "rep"), None),
        P(),
        P("rows", "rep", None),
        P("rows", "rep", None, None, None),
        P("rows", None),
    )
    return jax.shard_map(
        functools.partial(on_device, mesh.shape["rows"]),
        mesh=mesh,
        in_specs=placed,
        out_specs=(P(("rows", "rep"), None), P(("rows", "rep"), None), P()),
        check_vma=False,
    )
```

```python
import functools
import math

import jax
import jax.numpy as jnp
from jax import lax
from jax.experimental import pallas as pl
from jax.experimental.pallas import tpu as pltpu
from jax.sharding import PartitionSpec as P

F32 = jnp.float32
BF16 = jnp.bfloat16
HALF = 128
SCALE = 2.0**-21
VMEM = pl.BlockSpec(memory_space=pltpu.VMEM)
SMEM = pl.BlockSpec(memory_space=pltpu.SMEM)


def ring_order(n):
    return list(range(0, n, 2)) + list(range(n - 1, 0, -2))


def ring_place(i, n):
    return jnp.where(i % 2 == 0, i // 2, n - 1 - i // 2)


def split_dot(left, right, dims):
    high = left.astype(BF16)
    low = (left - high.astype(F32)).astype(BF16)
    out = lax.dot_general(high, right, (dims, ((), ())), preferred_element_type=F32)
    return out + lax.dot_general(low, right, (dims, ((), ())), preferred_element_type=F32)


def tie(arrays, other):
    return lax.optimization_barrier((arrays, other))[0]


def ring_ways(n):
    order = ring_order(n)
    ahead = [(order[i], order[(i + 1) % n]) for i in range(n)]
    return ahead, [(b, a) for a, b in ahead]


def gather_kernel(n, own_blocks, block, scale, where_ref, rep_ref, vals_ref, *refs):
    pieces, (send, keep_far, keep_near, pool) = refs[: n + 1], refs[n + 1 :]
    rows, half = own_blocks * block, n // 2
    starts = [p * rows for p in range(half + 1)] + [half * rows + rows // 2]
    starts += [p * rows for p in range(half + 1, n)]
    for start, ref in zip(starts, pieces):
        piece = ref[: min(ref.shape[0], rows), :]
        pool[start : start + piece.shape[0], :] = piece if scale is None else piece * jnp.asarray(scale, BF16)
    me = rep_ref[0]
    for mask, out, first in ((3, send, 0), (1, send, own_blocks), (2, keep_far, 0), (0, keep_near, 0)):
        base = lax.bitwise_xor(me, mask) * own_blocks
        for j in range(own_blocks):
            total = None
            for s in range(2):
                item = (base + j) * 2 + s
                start = pl.multiple_of(where_ref[item] * block, block)
                term = jnp.dot(vals_ref[item], pool[pl.ds(start, block), :], preferred_element_type=F32)
                total = term if total is None else total + term
            out[(first + j) * block : (first + j + 1) * block, :] = total.astype(out.dtype)


def gather_blocks(where, rep, vals, pieces, n, own_blocks, scale):
    block = vals.shape[-1]
    rows, width = pieces[0].shape
    shapes = [jax.ShapeDtypeStruct((2 * rows, width), BF16)]
    shapes += [jax.ShapeDtypeStruct((rows, width), F32)] * 2
    size = vals.size * 2 + 2 * n * rows * width * 2 + rows * width * 12
    return pl.pallas_call(
        functools.partial(gather_kernel, n, own_blocks, block, scale),
        out_shape=shapes,
        in_specs=[SMEM, SMEM, VMEM] + [VMEM] * (n + 1),
        out_specs=[VMEM] * 3,
        scratch_shapes=[pltpu.VMEM((n * rows, width), BF16)],
        compiler_params=pltpu.CompilerParams(vmem_limit_bytes=size + (8 << 20)),
        cost_estimate=pl.CostEstimate(
            flops=200 * vals.size * width, bytes_accessed=size, transcendentals=0
        ),
        name="gather_blocks",
    )(where, rep, vals, *pieces)


def scatter_kernel(own_blocks, block, scale, where_ref, rep_ref, vals_ref, *refs):
    sources, (own_ref, out_ref) = refs[:4], refs[4:]
    rows = own_blocks * block
    out_ref[...] = jnp.zeros_like(out_ref)
    me = rep_ref[0]
    for mask in range(4):
        base = lax.bitwise_xor(me, mask) * own_blocks
        for j in range(own_blocks):
            source = sources[mask][j * block : (j + 1) * block, :]
            if scale is not None:
                source = source * jnp.asarray(scale, BF16)
            for s in range(2):
                item = (base + j) * 2 + s
                start = pl.multiple_of(where_ref[item] * block, block)
                term = lax.dot_general(vals_ref[item], source, (((0,), (0,)), ((), ())), preferred_element_type=F32)
                out_ref[pl.ds(start, block), :] += term
    own_ref[...] = out_ref[:rows, :]


def scatter_blocks(where, rep, vals, sources, n, own_blocks, scale):
    block = vals.shape[-1]
    rows, width = sources[0].shape
    size = vals.size * 2 + 4 * rows * width * 2 + (n + 1) * rows * width * 4
    return pl.pallas_call(
        functools.partial(scatter_kernel, own_blocks, block, scale),
        out_shape=[jax.ShapeDtypeStruct((rows, width), F32), jax.ShapeDtypeStruct((n * rows, width), F32)],
        in_specs=[SMEM, SMEM, VMEM] + [VMEM] * 4,
        out_specs=[VMEM] * 2,
        compiler_params=pltpu.CompilerParams(vmem_limit_bytes=size + (4 << 20)),
        cost_estimate=pl.CostEstimate(
            flops=2 * vals.size * width, bytes_accessed=size, transcendentals=0
        ),
        name="scatter_blocks",
    )(where, rep, vals, *sources)


def add_terms(pair, terms, sent, riders):
    rows = terms[0].shape[0]
    mid = rows // 2
    size = pair[0].shape[0] - riders
    right, left = (array[:size].astype(F32) for array in pair)
    if size == mid:
        right = jnp.concatenate([terms[0][:mid] + right, terms[0][mid:]], 0)
        left = jnp.concatenate([terms[1][:mid], terms[1][mid:] + left], 0)
    else:
        right, left = terms[0] + right, terms[1] + left
    return tuple(
        jnp.concatenate([array.astype(sent), came[size:]], 0) if riders else array.astype(sent)
        for array, came in zip((right, left), pair)
    )


def spread(first, second, n, own_blocks, numbers, vals, scale, hooks):
    ahead, behind = ring_ways(n)
    rows, half = first.shape[0], n // 2
    mid = rows // 2
    sent = BF16 if n <= 8 else F32
    pairs = [[(i, i ^ mask) for i in range(4)] for mask in range(4)]
    hook = lambda name, after: hooks[name](after) if name in hooks else ()
    step = lambda pair: (lax.ppermute(pair[0], "rows", ahead), lax.ppermute(pair[1], "rows", behind))

    across = lax.ppermute(second, "rep", pairs[2])
    beside = lax.ppermute(tie(second, hook("beside", ())), "rep", pairs[1])
    gathered = step((first, first))
    pieces = [first] + [None] * n
    pieces[1], pieces[n] = gathered
    moving, riders, arrived = None, 0, []
    for hop in range(2, half + 1):
        if hop == 2:
            gathered = tie(gathered, (across, hook("gather 2", across)))
            far = lax.ppermute(across, "rep", pairs[1])
        else:
            gathered = tie(gathered, (moving, hook("gather %d" % hop, moving)))
        if hop == half:
            gathered = gathered[0][:mid], gathered[1][mid:rows]
        elif riders:
            gathered = tuple(jnp.concatenate([array[:rows], rider.astype(array.dtype)], 0) for array in gathered)
        behind_it = gathered
        gathered = step(gathered)
        pieces[hop], pieces[n + 1 - hop] = gathered
        if hop == 2:
            where, rep = numbers()
            sources = tie([second, beside, across, far], behind_it)
            own, partial = scatter_blocks(where, rep, vals, sources, n, own_blocks, scale)
            term = lambda distance: partial[distance * rows : (distance + 1) * rows]
            moving = term(half)[:mid].astype(sent), term(half)[mid:].astype(sent)
            if "riders" in hooks:
                rider = hooks["riders"](behind_it).astype(sent)
                riders = rider.shape[0]
                moving = tuple(jnp.concatenate([array, rider], 0) for array in moving)
        else:
            came = step(moving)
            arrived.append(came)
            moving = add_terms(came, (term(half + hop - 2), term(half - hop + 2)), sent, riders)
            moving = tie(moving, behind_it)
    pieces = tie(pieces, moving)
    *summed, crossing = reduce_rep(gather_blocks(where, rep, vals, pieces, n, own_blocks, scale))
    came = step(moving)
    arrived.append(came)
    moving = add_terms([array[:rows] for array in came], (term(n - 1), term(1)), sent, 0)
    if riders:
        moving = jnp.concatenate([moving[0], came[0][rows:]], 0), moving[1]
    moving = tie(moving, crossing)
    right, left = step(moving)
    arrived.append((right, None))
    return [*summed, own, right, left], arrived


def reduce_rep(parts):
    send, keep_far, keep_near = parts
    got = lax.ppermute(send, "rep", [(i, i ^ 1) for i in range(4)])
    crossing = (keep_far + got[: keep_far.shape[0]].astype(F32)).astype(BF16)
    return keep_near, got, lax.ppermute(crossing, "rep", [(i, i ^ 2) for i in range(4)]), crossing


def joined(refs):
    near, got, cross, own, right, left = refs
    rows = near.shape[0]
    first = near[...] + got[rows:, :].astype(F32) + cross[...].astype(F32)
    second = own[...] + (right[:rows, :].astype(F32) + left[...].astype(F32))
    return jnp.concatenate([first, second], axis=1)


def middle_kernel(rep_ref, weight_ref, grad_ref, *refs):
    sums, (act_ref, high_ref, low_ref, *masked_refs, grad, sem) = refs[:6], refs[6:]
    rows = act_ref.shape[0]
    start = pl.multiple_of(rep_ref[0] * rows, rows)
    copy = pltpu.make_async_copy(grad_ref.at[pl.ds(start, rows), :], grad, sem)
    copy.start()
    held = joined(sums)
    high = held.astype(BF16)
    low = (held - high.astype(F32)).astype(BF16)
    high_ref[...] = high
    low_ref[...] = low
    weight = weight_ref[...]
    summed = jnp.dot(high, weight, preferred_element_type=F32)
    summed = (summed + jnp.dot(low, weight, preferred_element_type=F32)) * (1.0 / SCALE)
    gate = jax.nn.sigmoid(summed)
    act_ref[...] = (summed * gate).astype(BF16)
    slope = gate * (1.0 + summed * (1.0 - gate))
    copy.wait()
    masked = (grad[...].astype(F32) * slope).astype(BF16)
    for h, ref in enumerate(masked_refs):
        ref[...] = masked[:, h * HALF : (h + 1) * HALF]


def middle(rep, weight, grad, sums):
    rows, width = sums[0].shape[0], grad.shape[1]
    shapes = [jax.ShapeDtypeStruct((rows, width), BF16)] * 3
    shapes += [jax.ShapeDtypeStruct((rows, HALF), BF16)] * (width // HALF)
    return pl.pallas_call(
        middle_kernel,
        out_shape=shapes,
        in_specs=[SMEM, VMEM, pl.BlockSpec(memory_space=pl.ANY)] + [VMEM] * 6,
        out_specs=[VMEM] * len(shapes),
        scratch_shapes=[pltpu.VMEM((rows, width), BF16), pltpu.SemaphoreType.DMA],
        compiler_params=pltpu.CompilerParams(vmem_limit_bytes=16 << 20),
        cost_estimate=pl.CostEstimate(
            flops=4 * rows * width * width, bytes_accessed=rows * width * 18, transcendentals=rows * width
        ),
        name="middle",
    )(rep, weight, grad, *sums)


def last_kernel(weight_ref, *refs):
    back = joined(refs[:6])
    refs[6][...] = split_dot(back, weight_ref[...], ((1,), (1,))).astype(BF16)


def last(weight, sums):
    rows, width = sums[0].shape[0], weight.shape[0]
    return pl.pallas_call(
        last_kernel,
        out_shape=jax.ShapeDtypeStruct((rows, width), BF16),
        in_specs=[VMEM] * 7,
        out_specs=VMEM,
        compiler_params=pltpu.CompilerParams(vmem_limit_bytes=24 << 20),
        cost_estimate=pl.CostEstimate(
            flops=4 * rows * width * width, bytes_accessed=rows * width * 14, transcendentals=0
        ),
        name="last",
    )(weight, *sums)


def local_kernel(rep_ref, high_ref, low_ref, *refs):
    masked, outs = refs[:2], refs[2:6]
    total = refs[6]
    for h, ref in enumerate(masked):
        part = None
        for held in (high_ref, low_ref):
            term = lax.dot_general(held[...], ref[...], (((0,), (0,)), ((), ())), preferred_element_type=F32)
            part = term if part is None else part + term
        total[h] = part
    rows = outs[0].shape[0] // 2
    for mask, out in enumerate(outs):
        start = pl.multiple_of(lax.bitwise_xor(rep_ref[0], mask) * rows, rows)
        for h in range(2):
            out[h * rows : (h + 1) * rows, :] = total[h, pl.ds(start, rows), :]


def local_grad(rep, high, low, masked):
    rows, width = high.shape
    return pl.pallas_call(
        local_kernel,
        out_shape=[jax.ShapeDtypeStruct((width // 2, HALF), F32)] * 4,
        in_specs=[SMEM] + [VMEM] * 4,
        out_specs=[VMEM] * 4,
        scratch_shapes=[pltpu.VMEM((2, width, HALF), F32)],
        compiler_params=pltpu.CompilerParams(vmem_limit_bytes=16 << 20),
        cost_estimate=pl.CostEstimate(
            flops=4 * rows * width * width, bytes_accessed=rows * width * 6, transcendentals=0
        ),
        name="local_grad",
    )(rep, high, low, *masked)


def round_kernel(n, spot_ref, *refs):
    held, out_ref, slots = refs[:n], refs[n], refs[n + 1]
    rows = out_ref.shape[0]
    for distance, ref in enumerate(held):
        slots[lax.rem(spot_ref[0] + distance, n)] = ref[ref.shape[0] - rows :, :].astype(F32)
    total = slots[0]
    for i in range(1, n):
        total = total + slots[i]
    out_ref[...] = total


def round_sum(spot, held):
    n, shape = len(held), held[0].shape
    return pl.pallas_call(
        functools.partial(round_kernel, n),
        out_shape=jax.ShapeDtypeStruct(shape, F32),
        in_specs=[SMEM] + [VMEM] * n,
        out_specs=VMEM,
        scratch_shapes=[pltpu.VMEM((n, *shape), F32)],
        compiler_params=pltpu.CompilerParams(vmem_limit_bytes=(2 * n + 8) << 17),
        name="round_sum",
    )(spot, *held)


def whole_kernel(scale, rep_ref, *refs):
    rows = refs[0].shape[0] // 2
    for mask in range(4):
        start = pl.multiple_of(lax.bitwise_xor(rep_ref[0], mask) * rows, rows)
        for h in range(2):
            part = refs[mask][h * rows : (h + 1) * rows, :] * scale
            refs[4][pl.ds(start, rows), h * HALF : (h + 1) * HALF] = part


def whole_grad(rep, quarters, scale):
    size = 2 * quarters[0].shape[0]
    return pl.pallas_call(
        functools.partial(whole_kernel, scale),
        out_shape=jax.ShapeDtypeStruct((size, 2 * HALF), F32),
        in_specs=[SMEM] + [VMEM] * 4,
        out_specs=VMEM,
        compiler_params=pltpu.CompilerParams(vmem_limit_bytes=4 << 20),
        name="whole_grad",
    )(rep, *quarters)


class GradientSum:
    def __init__(self, rep, spot, high, low, masked, n, scale):
        self.rep, self.spot, self.local, self.n, self.scale = rep, spot, (high, low, masked), n, scale
        self.pairs = [[(i, i ^ mask) for i in range(4)] for mask in range(4)]

    def start(self, after):
        high, low, masked = tie(self.local, after)
        self.quarters = local_grad(self.rep, high, low, masked)
        return self.quarters

    def riders(self, after):
        value = self.quarters[0]
        for mask in (1, 2, 3):
            value = value + lax.ppermute(self.quarters[mask], "rep", self.pairs[mask])
        self.value = value.astype(BF16)
        return self.value

    def finish(self, arrived):
        held = [self.value] + [None] * (self.n - 1)
        for hop, (right, left) in enumerate(arrived, 1):
            held[self.n - hop] = right
            if left is not None:
                held[hop] = left
        value = round_sum(self.spot, held)
        others = [lax.ppermute(value, "rep", self.pairs[mask]) for mask in (1, 2, 3)]
        return whole_grad(self.rep, [value, *others], self.scale)


def on_device(n, features, weight, block_cols, block_vals, out_grad):
    own_rows, width = features.shape
    block = block_vals.shape[-1]
    own_blocks = own_rows // block
    me, layer = lax.axis_index("rows"), lax.axis_index("rep")
    vals = block_vals.reshape(-1, block, block)
    chunks = [features[:, h * HALF : (h + 1) * HALF] for h in range(width // HALF)]
    ready = {}

    def prepared(after):
        my, rep, cols = tie((me.astype(jnp.int32), layer.astype(jnp.int32).reshape(1), block_cols), after)
        cols = cols.reshape(-1)
        back_steps = (ring_place(my, n) - ring_place(cols // own_blocks, n) + n) % n
        ready["spot"] = ring_place(my, n).reshape(1)
        ready["rep"], ready["where"] = rep, back_steps * own_blocks + cols % own_blocks
        return ready["rep"], ready["where"], ready["spot"]

    numbers = lambda: (ready["where"], ready["rep"])
    sums, _ = spread(*chunks, n, own_blocks, numbers, vals, SCALE, {"beside": prepared})
    rep = ready["rep"]
    activated, high, low, *masked = middle(rep, weight, out_grad, sums)

    node_total = own_rows * n * 4
    grad = GradientSum(rep, ready["spot"], high, low, masked, n, 1.0 / (SCALE * math.sqrt(node_total)))
    sums, arrived = spread(*masked, n, own_blocks, numbers, vals, None, {"gather 2": grad.start, "riders": grad.riders})
    weight_grad = grad.finish(arrived)
    input_grad = last(weight, sums)
    return activated, input_grad, weight_grad


def solution(mesh):
    placed = (
        P(("rows", "rep"), None),
        P(),
        P("rows", "rep", None),
        P("rows", "rep", None, None, None),
        P("rows", None),
    )
    return jax.shard_map(
        functools.partial(on_device, mesh.shape["rows"]),
        mesh=mesh,
        in_specs=placed,
        out_specs=(P(("rows", "rep"), None), P(("rows", "rep"), None), P()),
        check_vma=False,
    )
```

```python
import functools
import math

import jax
import jax.numpy as jnp
from jax import lax
from jax.experimental import pallas as pl
from jax.experimental.pallas import tpu as pltpu
from jax.sharding import PartitionSpec as P

F32 = jnp.float32
BF16 = jnp.bfloat16
HALF = 128
SCALE = 2.0**-21
VMEM = pl.BlockSpec(memory_space=pltpu.VMEM)
SMEM = pl.BlockSpec(memory_space=pltpu.SMEM)


def ring_order(n):
    return list(range(0, n, 2)) + list(range(n - 1, 0, -2))


def ring_place(i, n):
    return jnp.where(i % 2 == 0, i // 2, n - 1 - i // 2)


def split_dot(left, right, dims):
    high = left.astype(BF16)
    low = (left - high.astype(F32)).astype(BF16)
    out = lax.dot_general(high, right, (dims, ((), ())), preferred_element_type=F32)
    return out + lax.dot_general(low, right, (dims, ((), ())), preferred_element_type=F32)


def tie(arrays, other):
    return lax.optimization_barrier((arrays, other))[0]


def ring_ways(n):
    order = ring_order(n)
    ahead = [(order[i], order[(i + 1) % n]) for i in range(n)]
    return ahead, [(b, a) for a, b in ahead]


def gather_kernel(n, own_blocks, block, scale, where_ref, rep_ref, vals_ref, *refs):
    pieces, (send, keep_far, keep_near, pool) = refs[: n + 1], refs[n + 1 :]
    rows, half = own_blocks * block, n // 2
    starts = [p * rows for p in range(half + 1)] + [half * rows + rows // 2]
    starts += [p * rows for p in range(half + 1, n)]
    for start, ref in zip(starts, pieces):
        piece = ref[: min(ref.shape[0], rows), :]
        pool[start : start + piece.shape[0], :] = piece if scale is None else piece * jnp.asarray(scale, BF16)
    me = rep_ref[0]
    for mask, out, first in ((3, send, 0), (1, send, own_blocks), (2, keep_far, 0), (0, keep_near, 0)):
        base = lax.bitwise_xor(me, mask) * own_blocks
        for j in range(own_blocks):
            total = None
            for s in range(2):
                item = (base + j) * 2 + s
                start = pl.multiple_of(where_ref[item] * block, block)
                term = jnp.dot(vals_ref[item], pool[pl.ds(start, block), :], preferred_element_type=F32)
                total = term if total is None else total + term
            out[(first + j) * block : (first + j + 1) * block, :] = total.astype(out.dtype)


def gather_blocks(where, rep, vals, pieces, n, own_blocks, scale):
    block = vals.shape[-1]
    rows, width = pieces[0].shape
    shapes = [jax.ShapeDtypeStruct((2 * rows, width), BF16)]
    shapes += [jax.ShapeDtypeStruct((rows, width), F32)] * 2
    size = vals.size * 2 + 2 * n * rows * width * 2 + rows * width * 12
    return pl.pallas_call(
        functools.partial(gather_kernel, n, own_blocks, block, scale),
        out_shape=shapes,
        in_specs=[SMEM, SMEM, VMEM] + [VMEM] * (n + 1),
        out_specs=[VMEM] * 3,
        scratch_shapes=[pltpu.VMEM((n * rows, width), BF16)],
        compiler_params=pltpu.CompilerParams(vmem_limit_bytes=size + (8 << 20)),
        cost_estimate=pl.CostEstimate(
            flops=200 * vals.size * width, bytes_accessed=size, transcendentals=0
        ),
        name="gather_blocks",
    )(where, rep, vals, *pieces)


def scatter_kernel(own_blocks, block, scale, where_ref, rep_ref, vals_ref, *refs):
    sources, (own_ref, out_ref) = refs[:4], refs[4:]
    rows = own_blocks * block
    out_ref[...] = jnp.zeros_like(out_ref)
    me = rep_ref[0]
    for mask in range(4):
        base = lax.bitwise_xor(me, mask) * own_blocks
        for j in range(own_blocks):
            source = sources[mask][j * block : (j + 1) * block, :]
            if scale is not None:
                source = source * jnp.asarray(scale, BF16)
            for s in range(2):
                item = (base + j) * 2 + s
                start = pl.multiple_of(where_ref[item] * block, block)
                term = lax.dot_general(vals_ref[item], source, (((0,), (0,)), ((), ())), preferred_element_type=F32)
                out_ref[pl.ds(start, block), :] += term
    own_ref[...] = out_ref[:rows, :]


def scatter_blocks(where, rep, vals, sources, n, own_blocks, scale):
    block = vals.shape[-1]
    rows, width = sources[0].shape
    size = vals.size * 2 + 4 * rows * width * 2 + (n + 1) * rows * width * 4
    return pl.pallas_call(
        functools.partial(scatter_kernel, own_blocks, block, scale),
        out_shape=[jax.ShapeDtypeStruct((rows, width), F32), jax.ShapeDtypeStruct((n * rows, width), F32)],
        in_specs=[SMEM, SMEM, VMEM] + [VMEM] * 4,
        out_specs=[VMEM] * 2,
        compiler_params=pltpu.CompilerParams(vmem_limit_bytes=size + (4 << 20)),
        cost_estimate=pl.CostEstimate(
            flops=2 * vals.size * width, bytes_accessed=size, transcendentals=0
        ),
        name="scatter_blocks",
    )(where, rep, vals, *sources)


def near_kernel(vals_ref, out_ref, sem):
    copy = pltpu.make_async_copy(vals_ref, out_ref, sem)
    copy.start()
    copy.wait()


def brought_near(vals):
    return pl.pallas_call(
        near_kernel,
        out_shape=jax.ShapeDtypeStruct(vals.shape, vals.dtype),
        in_specs=[pl.BlockSpec(memory_space=pl.ANY)],
        out_specs=VMEM,
        scratch_shapes=[pltpu.SemaphoreType.DMA],
        compiler_params=pltpu.CompilerParams(vmem_limit_bytes=4 << 20),
        name="brought_near",
    )(vals)


def add_terms(pair, terms, sent, riders):
    rows = terms[0].shape[0]
    mid = rows // 2
    size = pair[0].shape[0] - riders
    right, left = (array[:size].astype(F32) for array in pair)
    if size == mid:
        right = jnp.concatenate([terms[0][:mid] + right, terms[0][mid:]], 0)
        left = jnp.concatenate([terms[1][:mid], terms[1][mid:] + left], 0)
    else:
        right, left = terms[0] + right, terms[1] + left
    return tuple(
        jnp.concatenate([array.astype(sent), came[size:]], 0) if riders else array.astype(sent)
        for array, came in zip((right, left), pair)
    )


def spread(first, second, n, own_blocks, numbers, scale, hooks):
    ahead, behind = ring_ways(n)
    rows, half = first.shape[0], n // 2
    mid = rows // 2
    sent = BF16 if n <= 8 else F32
    pairs = [[(i, i ^ mask) for i in range(4)] for mask in range(4)]
    hook = lambda name, after: hooks[name](after) if name in hooks else ()
    step = lambda pair: (lax.ppermute(pair[0], "rows", ahead), lax.ppermute(pair[1], "rows", behind))

    across = lax.ppermute(second, "rep", pairs[2])
    beside = lax.ppermute(tie(second, hook("beside", ())), "rep", pairs[1])
    gathered = step((first, first))
    pieces = [first] + [None] * n
    pieces[1], pieces[n] = gathered
    moving, riders, arrived = None, 0, []
    for hop in range(2, half + 1):
        if hop == 2:
            gathered = tie(gathered, (across, hook("gather 2", across)))
            far = lax.ppermute(across, "rep", pairs[1])
        else:
            gathered = tie(gathered, (moving, hook("gather %d" % hop, moving)))
        if hop == half:
            gathered = gathered[0][:mid], gathered[1][mid:rows]
        elif riders:
            gathered = tuple(jnp.concatenate([array[:rows], rider.astype(array.dtype)], 0) for array in gathered)
        behind_it = gathered
        gathered = step(gathered)
        pieces[hop], pieces[n + 1 - hop] = gathered
        if hop == 2:
            where, rep, vals = numbers()
            sources = tie([second, beside, across, far], behind_it)
            own, partial = scatter_blocks(where, rep, vals, sources, n, own_blocks, scale)
            term = lambda distance: partial[distance * rows : (distance + 1) * rows]
            moving = term(half)[:mid].astype(sent), term(half)[mid:].astype(sent)
            if "riders" in hooks:
                rider = hooks["riders"](behind_it).astype(sent)
                riders = rider.shape[0]
                moving = tuple(jnp.concatenate([array, rider], 0) for array in moving)
        else:
            came = step(moving)
            arrived.append(came)
            moving = add_terms(came, (term(half + hop - 2), term(half - hop + 2)), sent, riders)
            moving = tie(moving, behind_it)
    pieces = tie(pieces, moving)
    *summed, crossing = reduce_rep(gather_blocks(where, rep, vals, pieces, n, own_blocks, scale))
    came = step(moving)
    arrived.append(came)
    moving = add_terms([array[:rows] for array in came], (term(n - 1), term(1)), sent, 0)
    if riders:
        moving = jnp.concatenate([moving[0], came[0][rows:]], 0), moving[1]
    moving = tie(moving, crossing)
    right, left = step(moving)
    arrived.append((right, None))
    return [*summed, own, right, left], arrived


def reduce_rep(parts):
    send, keep_far, keep_near = parts
    got = lax.ppermute(send, "rep", [(i, i ^ 1) for i in range(4)])
    crossing = (keep_far + got[: keep_far.shape[0]].astype(F32)).astype(BF16)
    return keep_near, got, lax.ppermute(crossing, "rep", [(i, i ^ 2) for i in range(4)]), crossing


def joined(refs):
    near, got, cross, own, right, left = refs
    rows = near.shape[0]
    first = near[...] + got[rows:, :].astype(F32) + cross[...].astype(F32)
    second = own[...] + (right[:rows, :].astype(F32) + left[...].astype(F32))
    return jnp.concatenate([first, second], axis=1)


def middle_kernel(rep_ref, weight_ref, grad_ref, *refs):
    sums, (act_ref, high_ref, low_ref, *masked_refs, grad, sem) = refs[:6], refs[6:]
    rows = act_ref.shape[0]
    start = pl.multiple_of(rep_ref[0] * rows, rows)
    copy = pltpu.make_async_copy(grad_ref.at[pl.ds(start, rows), :], grad, sem)
    copy.start()
    held = joined(sums)
    high = held.astype(BF16)
    low = (held - high.astype(F32)).astype(BF16)
    high_ref[...] = high
    low_ref[...] = low
    weight = weight_ref[...]
    summed = jnp.dot(high, weight, preferred_element_type=F32)
    summed = (summed + jnp.dot(low, weight, preferred_element_type=F32)) * (1.0 / SCALE)
    gate = jax.nn.sigmoid(summed)
    act_ref[...] = (summed * gate).astype(BF16)
    slope = gate * (1.0 + summed * (1.0 - gate))
    copy.wait()
    masked = (grad[...].astype(F32) * slope).astype(BF16)
    for h, ref in enumerate(masked_refs):
        ref[...] = masked[:, h * HALF : (h + 1) * HALF]


def middle(rep, weight, grad, sums):
    rows, width = sums[0].shape[0], grad.shape[1]
    shapes = [jax.ShapeDtypeStruct((rows, width), BF16)] * 3
    shapes += [jax.ShapeDtypeStruct((rows, HALF), BF16)] * (width // HALF)
    return pl.pallas_call(
        middle_kernel,
        out_shape=shapes,
        in_specs=[SMEM, VMEM, pl.BlockSpec(memory_space=pl.ANY)] + [VMEM] * 6,
        out_specs=[VMEM] * len(shapes),
        scratch_shapes=[pltpu.VMEM((rows, width), BF16), pltpu.SemaphoreType.DMA],
        compiler_params=pltpu.CompilerParams(vmem_limit_bytes=16 << 20),
        cost_estimate=pl.CostEstimate(
            flops=4 * rows * width * width, bytes_accessed=rows * width * 18, transcendentals=rows * width
        ),
        name="middle",
    )(rep, weight, grad, *sums)


def last_kernel(weight_ref, *refs):
    back = joined(refs[:6])
    refs[6][...] = split_dot(back, weight_ref[...], ((1,), (1,))).astype(BF16)


def last(weight, sums):
    rows, width = sums[0].shape[0], weight.shape[0]
    return pl.pallas_call(
        last_kernel,
        out_shape=jax.ShapeDtypeStruct((rows, width), BF16),
        in_specs=[VMEM] * 7,
        out_specs=VMEM,
        compiler_params=pltpu.CompilerParams(vmem_limit_bytes=24 << 20),
        cost_estimate=pl.CostEstimate(
            flops=4 * rows * width * width, bytes_accessed=rows * width * 14, transcendentals=0
        ),
        name="last",
    )(weight, *sums)


def local_kernel(rep_ref, high_ref, low_ref, *refs):
    masked, outs = refs[:2], refs[2:6]
    total = refs[6]
    for h, ref in enumerate(masked):
        part = None
        for held in (high_ref, low_ref):
            term = lax.dot_general(held[...], ref[...], (((0,), (0,)), ((), ())), preferred_element_type=F32)
            part = term if part is None else part + term
        total[h] = part
    rows = outs[0].shape[0] // 2
    for mask, out in enumerate(outs):
        start = pl.multiple_of(lax.bitwise_xor(rep_ref[0], mask) * rows, rows)
        for h in range(2):
            out[h * rows : (h + 1) * rows, :] = total[h, pl.ds(start, rows), :]


def local_grad(rep, high, low, masked):
    rows, width = high.shape
    return pl.pallas_call(
        local_kernel,
        out_shape=[jax.ShapeDtypeStruct((width // 2, HALF), F32)] * 4,
        in_specs=[SMEM] + [VMEM] * 4,
        out_specs=[VMEM] * 4,
        scratch_shapes=[pltpu.VMEM((2, width, HALF), F32)],
        compiler_params=pltpu.CompilerParams(vmem_limit_bytes=16 << 20),
        cost_estimate=pl.CostEstimate(
            flops=4 * rows * width * width, bytes_accessed=rows * width * 6, transcendentals=0
        ),
        name="local_grad",
    )(rep, high, low, *masked)


def round_kernel(n, spot_ref, *refs):
    held, out_ref, slots = refs[:n], refs[n], refs[n + 1]
    rows = out_ref.shape[0]
    for distance, ref in enumerate(held):
        slots[lax.rem(spot_ref[0] + distance, n)] = ref[ref.shape[0] - rows :, :].astype(F32)
    total = slots[0]
    for i in range(1, n):
        total = total + slots[i]
    out_ref[...] = total


def round_sum(spot, held):
    n, shape = len(held), held[0].shape
    return pl.pallas_call(
        functools.partial(round_kernel, n),
        out_shape=jax.ShapeDtypeStruct(shape, F32),
        in_specs=[SMEM] + [VMEM] * n,
        out_specs=VMEM,
        scratch_shapes=[pltpu.VMEM((n, *shape), F32)],
        compiler_params=pltpu.CompilerParams(vmem_limit_bytes=(2 * n + 8) << 17),
        name="round_sum",
    )(spot, *held)


def whole_kernel(scale, rep_ref, *refs):
    rows = refs[0].shape[0] // 2
    for mask in range(4):
        start = pl.multiple_of(lax.bitwise_xor(rep_ref[0], mask) * rows, rows)
        for h in range(2):
            part = refs[mask][h * rows : (h + 1) * rows, :] * scale
            refs[4][pl.ds(start, rows), h * HALF : (h + 1) * HALF] = part


def whole_grad(rep, quarters, scale):
    size = 2 * quarters[0].shape[0]
    return pl.pallas_call(
        functools.partial(whole_kernel, scale),
        out_shape=jax.ShapeDtypeStruct((size, 2 * HALF), F32),
        in_specs=[SMEM] + [VMEM] * 4,
        out_specs=VMEM,
        compiler_params=pltpu.CompilerParams(vmem_limit_bytes=4 << 20),
        name="whole_grad",
    )(rep, *quarters)


class GradientSum:
    def __init__(self, rep, spot, high, low, masked, n, scale):
        self.rep, self.spot, self.local, self.n, self.scale = rep, spot, (high, low, masked), n, scale
        self.pairs = [[(i, i ^ mask) for i in range(4)] for mask in range(4)]

    def start(self, after):
        high, low, masked = tie(self.local, after)
        self.quarters = local_grad(self.rep, high, low, masked)
        return self.quarters

    def riders(self, after):
        value = self.quarters[0]
        for mask in (1, 2, 3):
            value = value + lax.ppermute(self.quarters[mask], "rep", self.pairs[mask])
        self.value = value.astype(BF16)
        return self.value

    def finish(self, arrived):
        held = [self.value] + [None] * (self.n - 1)
        for hop, (right, left) in enumerate(arrived, 1):
            held[self.n - hop] = right
            if left is not None:
                held[hop] = left
        value = round_sum(self.spot, held)
        others = [lax.ppermute(value, "rep", self.pairs[mask]) for mask in (1, 2, 3)]
        return whole_grad(self.rep, [value, *others], self.scale)


def on_device(n, features, weight, block_cols, block_vals, out_grad):
    own_rows, width = features.shape
    block = block_vals.shape[-1]
    own_blocks = own_rows // block
    me, layer = lax.axis_index("rows"), lax.axis_index("rep")
    vals = block_vals.reshape(-1, block, block)
    chunks = [features[:, h * HALF : (h + 1) * HALF] for h in range(width // HALF)]
    ready = {}

    def prepared(after):
        my, rep, cols = tie((me.astype(jnp.int32), layer.astype(jnp.int32).reshape(1), block_cols), after)
        cols = cols.reshape(-1)
        back_steps = (ring_place(my, n) - ring_place(cols // own_blocks, n) + n) % n
        ready["spot"] = ring_place(my, n).reshape(1)
        ready["rep"], ready["where"] = rep, back_steps * own_blocks + cols % own_blocks
        ready["vals"] = brought_near(vals)
        return ready["rep"], ready["where"], ready["spot"], ready["vals"]

    numbers = lambda: (ready["where"], ready["rep"], ready["vals"])
    sums, _ = spread(*chunks, n, own_blocks, numbers, SCALE, {"beside": prepared})
    rep = ready["rep"]
    activated, high, low, *masked = middle(rep, weight, out_grad, sums)

    node_total = own_rows * n * 4
    grad = GradientSum(rep, ready["spot"], high, low, masked, n, 1.0 / (SCALE * math.sqrt(node_total)))
    sums, arrived = spread(*masked, n, own_blocks, numbers, None, {"gather 2": grad.start, "riders": grad.riders})
    weight_grad = grad.finish(arrived)
    input_grad = last(weight, sums)
    return activated, input_grad, weight_grad


def solution(mesh):
    placed = (
        P(("rows", "rep"), None),
        P(),
        P("rows", "rep", None),
        P("rows", "rep", None, None, None),
        P("rows", None),
    )
    return jax.shard_map(
        functools.partial(on_device, mesh.shape["rows"]),
        mesh=mesh,
        in_specs=placed,
        out_specs=(P(("rows", "rep"), None), P(("rows", "rep"), None), P()),
        check_vma=False,
    )
```

```python
import functools
import math

import jax
import jax.numpy as jnp
from jax import lax
from jax.experimental import pallas as pl
from jax.experimental.pallas import tpu as pltpu
from jax.sharding import PartitionSpec as P

F32 = jnp.float32
BF16 = jnp.bfloat16
HALF = 128
SCALE = 2.0**-21
VMEM = pl.BlockSpec(memory_space=pltpu.VMEM)
SMEM = pl.BlockSpec(memory_space=pltpu.SMEM)


def ring_order(n):
    return list(range(0, n, 2)) + list(range(n - 1, 0, -2))


def ring_place(i, n):
    return jnp.where(i % 2 == 0, i // 2, n - 1 - i // 2)


def split_dot(left, right, dims):
    high = left.astype(BF16)
    low = (left - high.astype(F32)).astype(BF16)
    out = lax.dot_general(high, right, (dims, ((), ())), preferred_element_type=F32)
    return out + lax.dot_general(low, right, (dims, ((), ())), preferred_element_type=F32)


def tie(arrays, other):
    return lax.optimization_barrier((arrays, other))[0]


def ring_ways(n):
    order = ring_order(n)
    ahead = [(order[i], order[(i + 1) % n]) for i in range(n)]
    return ahead, [(b, a) for a, b in ahead]


def gather_kernel(n, own_blocks, block, scale, where_ref, rep_ref, vals_ref, *refs):
    pieces, (send, keep_far, keep_near, pool) = refs[: n + 1], refs[n + 1 :]
    rows, half = own_blocks * block, n // 2
    starts = [p * rows for p in range(half + 1)] + [half * rows + rows // 2]
    starts += [p * rows for p in range(half + 1, n)]
    for start, ref in zip(starts, pieces):
        piece = ref[: min(ref.shape[0], rows), :]
        pool[start : start + piece.shape[0], :] = piece if scale is None else piece * jnp.asarray(scale, BF16)
    me = rep_ref[0]
    for mask, out, first in ((3, send, 0), (1, send, own_blocks), (2, keep_far, 0), (0, keep_near, 0)):
        base = lax.bitwise_xor(me, mask) * own_blocks
        for j in range(own_blocks):
            total = None
            for s in range(2):
                item = (base + j) * 2 + s
                start = pl.multiple_of(where_ref[item] * block, block)
                term = jnp.dot(vals_ref[item], pool[pl.ds(start, block), :], preferred_element_type=F32)
                total = term if total is None else total + term
            out[(first + j) * block : (first + j + 1) * block, :] = total.astype(out.dtype)


def gather_blocks(where, rep, vals, pieces, n, own_blocks, scale):
    block = vals.shape[-1]
    rows, width = pieces[0].shape
    shapes = [jax.ShapeDtypeStruct((2 * rows, width), BF16)]
    shapes += [jax.ShapeDtypeStruct((rows, width), F32)] * 2
    size = vals.size * 2 + 2 * n * rows * width * 2 + rows * width * 12
    return pl.pallas_call(
        functools.partial(gather_kernel, n, own_blocks, block, scale),
        out_shape=shapes,
        in_specs=[SMEM, SMEM, VMEM] + [VMEM] * (n + 1),
        out_specs=[VMEM] * 3,
        scratch_shapes=[pltpu.VMEM((n * rows, width), BF16)],
        compiler_params=pltpu.CompilerParams(vmem_limit_bytes=size + (8 << 20)),
        cost_estimate=pl.CostEstimate(
            flops=200 * vals.size * width, bytes_accessed=size, transcendentals=0
        ),
        name="gather_blocks",
    )(where, rep, vals, *pieces)


def scatter_kernel(own_blocks, block, scale, where_ref, rep_ref, vals_ref, *refs):
    sources, (own_ref, out_ref) = refs[:4], refs[4:]
    rows = own_blocks * block
    out_ref[...] = jnp.zeros_like(out_ref)
    me = rep_ref[0]
    for mask in range(4):
        base = lax.bitwise_xor(me, mask) * own_blocks
        for j in range(own_blocks):
            source = sources[mask][j * block : (j + 1) * block, :]
            if scale is not None:
                source = source * jnp.asarray(scale, BF16)
            for s in range(2):
                item = (base + j) * 2 + s
                start = pl.multiple_of(where_ref[item] * block, block)
                term = lax.dot_general(vals_ref[item], source, (((0,), (0,)), ((), ())), preferred_element_type=F32)
                out_ref[pl.ds(start, block), :] += term
    own_ref[...] = out_ref[:rows, :]


def scatter_blocks(where, rep, vals, sources, n, own_blocks, scale):
    block = vals.shape[-1]
    rows, width = sources[0].shape
    size = vals.size * 2 + 4 * rows * width * 2 + (n + 1) * rows * width * 4
    return pl.pallas_call(
        functools.partial(scatter_kernel, own_blocks, block, scale),
        out_shape=[jax.ShapeDtypeStruct((rows, width), F32), jax.ShapeDtypeStruct((n * rows, width), F32)],
        in_specs=[SMEM, SMEM, VMEM] + [VMEM] * 4,
        out_specs=[VMEM] * 2,
        compiler_params=pltpu.CompilerParams(vmem_limit_bytes=size + (4 << 20)),
        cost_estimate=pl.CostEstimate(
            flops=2 * vals.size * width, bytes_accessed=size, transcendentals=0
        ),
        name="scatter_blocks",
    )(where, rep, vals, *sources)


def near_kernel(vals_ref, out_ref, sem):
    copy = pltpu.make_async_copy(vals_ref, out_ref, sem)
    copy.start()
    copy.wait()


def brought_near(vals):
    return pl.pallas_call(
        near_kernel,
        out_shape=jax.ShapeDtypeStruct(vals.shape, vals.dtype),
        in_specs=[pl.BlockSpec(memory_space=pl.ANY)],
        out_specs=VMEM,
        scratch_shapes=[pltpu.SemaphoreType.DMA],
        compiler_params=pltpu.CompilerParams(vmem_limit_bytes=4 << 20),
        name="brought_near",
    )(vals)


def add_terms(pair, terms, sent, riders):
    rows = terms[0].shape[0]
    mid = rows // 2
    size = pair[0].shape[0] - riders
    right, left = (array[:size].astype(F32) for array in pair)
    if size == mid:
        right = jnp.concatenate([terms[0][:mid] + right, terms[0][mid:]], 0)
        left = jnp.concatenate([terms[1][:mid], terms[1][mid:] + left], 0)
    else:
        right, left = terms[0] + right, terms[1] + left
    return tuple(
        jnp.concatenate([array.astype(sent), came[size:]], 0) if riders else array.astype(sent)
        for array, came in zip((right, left), pair)
    )


def spread(first, second, n, own_blocks, numbers, scale, hooks):
    ahead, behind = ring_ways(n)
    rows, half = first.shape[0], n // 2
    mid = rows // 2
    sent = BF16 if n <= 8 else F32
    pairs = [[(i, i ^ mask) for i in range(4)] for mask in range(4)]
    hook = lambda name, after: hooks[name](after) if name in hooks else ()
    step = lambda pair: (lax.ppermute(pair[0], "rows", ahead), lax.ppermute(pair[1], "rows", behind))

    across = lax.ppermute(second, "rep", pairs[2])
    beside = lax.ppermute(tie(second, hook("beside", ())), "rep", pairs[1])
    gathered = step((first, first))
    pieces = [first] + [None] * n
    pieces[1], pieces[n] = gathered
    moving, riders, arrived = None, 0, []
    for hop in range(2, half + 1):
        if hop == 2:
            gathered = tie(gathered, (across, hook("gather 2", across)))
            far = lax.ppermute(across, "rep", pairs[1])
        else:
            gathered = tie(gathered, (moving, hook("gather %d" % hop, moving)))
        if hop == half:
            gathered = gathered[0][:mid], gathered[1][mid:rows]
        elif riders:
            gathered = tuple(jnp.concatenate([array[:rows], rider.astype(array.dtype)], 0) for array in gathered)
        behind_it = gathered
        gathered = step(gathered)
        pieces[hop], pieces[n + 1 - hop] = gathered
        if hop == 2:
            where, rep, vals = numbers()
            sources = tie([second, beside, across, far], behind_it)
            own, partial = scatter_blocks(where, rep, vals, sources, n, own_blocks, scale)
            term = lambda distance: partial[distance * rows : (distance + 1) * rows]
            moving = term(half)[:mid].astype(sent), term(half)[mid:].astype(sent)
            if "riders" in hooks:
                rider = hooks["riders"](behind_it).astype(sent)
                riders = rider.shape[0]
                moving = tuple(jnp.concatenate([array, rider], 0) for array in moving)
        else:
            came = step(moving)
            arrived.append(came)
            moving = add_terms(came, (term(half + hop - 2), term(half - hop + 2)), sent, riders)
            moving = tie(moving, behind_it)
    pieces = tie(pieces, moving)
    *summed, crossing = reduce_rep(gather_blocks(where, rep, vals, pieces, n, own_blocks, scale))
    came = step(moving)
    arrived.append(came)
    moving = add_terms([array[:rows] for array in came], (term(n - 1), term(1)), sent, 0)
    if riders:
        moving = jnp.concatenate([moving[0], came[0][rows:]], 0), moving[1]
    moving = tie(moving, crossing)
    right, left = step(moving)
    arrived.append((right, None))
    return [*summed, own, right, left], arrived


def reduce_rep(parts):
    send, keep_far, keep_near = parts
    got = lax.ppermute(send, "rep", [(i, i ^ 1) for i in range(4)])
    crossing = (keep_far + got[: keep_far.shape[0]].astype(F32)).astype(BF16)
    return keep_near, got, lax.ppermute(crossing, "rep", [(i, i ^ 2) for i in range(4)]), crossing


def joined(refs):
    near, got, cross, own, right, left = refs
    rows = near.shape[0]
    first = near[...] + got[rows:, :].astype(F32) + cross[...].astype(F32)
    second = own[...] + (right[:rows, :].astype(F32) + left[...].astype(F32))
    return jnp.concatenate([first, second], axis=1)


def middle_kernel(rep_ref, weight_ref, grad_ref, *refs):
    sums, (act_ref, high_ref, low_ref, *masked_refs, grad, sem) = refs[:6], refs[6:]
    rows = act_ref.shape[0]
    start = pl.multiple_of(rep_ref[0] * rows, rows)
    copy = pltpu.make_async_copy(grad_ref.at[pl.ds(start, rows), :], grad, sem)
    copy.start()
    held = joined(sums)
    high = held.astype(BF16)
    low = (held - high.astype(F32)).astype(BF16)
    high_ref[...] = high
    low_ref[...] = low
    weight = weight_ref[...]
    summed = jnp.dot(high, weight, preferred_element_type=F32)
    summed = (summed + jnp.dot(low, weight, preferred_element_type=F32)) * (1.0 / SCALE)
    gate = jax.nn.sigmoid(summed)
    act_ref[...] = (summed * gate).astype(BF16)
    slope = gate * (1.0 + summed * (1.0 - gate))
    copy.wait()
    masked = (grad[...].astype(F32) * slope).astype(BF16)
    for h, ref in enumerate(masked_refs):
        ref[...] = masked[:, h * HALF : (h + 1) * HALF]


def middle(rep, weight, grad, sums):
    rows, width = sums[0].shape[0], grad.shape[1]
    shapes = [jax.ShapeDtypeStruct((rows, width), BF16)] * 3
    shapes += [jax.ShapeDtypeStruct((rows, HALF), BF16)] * (width // HALF)
    return pl.pallas_call(
        middle_kernel,
        out_shape=shapes,
        in_specs=[SMEM, VMEM, pl.BlockSpec(memory_space=pl.ANY)] + [VMEM] * 6,
        out_specs=[VMEM] * len(shapes),
        scratch_shapes=[pltpu.VMEM((rows, width), BF16), pltpu.SemaphoreType.DMA],
        compiler_params=pltpu.CompilerParams(vmem_limit_bytes=16 << 20),
        cost_estimate=pl.CostEstimate(
            flops=4 * rows * width * width, bytes_accessed=rows * width * 18, transcendentals=rows * width
        ),
        name="middle",
    )(rep, weight, grad, *sums)


def last_kernel(weight_ref, *refs):
    back = joined(refs[:6])
    refs[6][...] = split_dot(back, weight_ref[...], ((1,), (1,))).astype(BF16)


def last(weight, sums):
    rows, width = sums[0].shape[0], weight.shape[0]
    return pl.pallas_call(
        last_kernel,
        out_shape=jax.ShapeDtypeStruct((rows, width), BF16),
        in_specs=[VMEM] * 7,
        out_specs=VMEM,
        compiler_params=pltpu.CompilerParams(vmem_limit_bytes=24 << 20),
        cost_estimate=pl.CostEstimate(
            flops=4 * rows * width * width, bytes_accessed=rows * width * 14, transcendentals=0
        ),
        name="last",
    )(weight, *sums)


def local_kernel(rep_ref, high_ref, low_ref, *refs):
    masked, outs = refs[:2], refs[2:6]
    total = refs[6]
    for h, ref in enumerate(masked):
        part = None
        for held in (high_ref, low_ref):
            term = lax.dot_general(held[...], ref[...], (((0,), (0,)), ((), ())), preferred_element_type=F32)
            part = term if part is None else part + term
        total[h] = part
    rows = outs[0].shape[0] // 2
    for mask, out in enumerate(outs):
        start = pl.multiple_of(lax.bitwise_xor(rep_ref[0], mask) * rows, rows)
        for h in range(2):
            out[h * rows : (h + 1) * rows, :] = total[h, pl.ds(start, rows), :].astype(out.dtype)


def local_grad(rep, high, low, masked):
    rows, width = high.shape
    return pl.pallas_call(
        local_kernel,
        out_shape=[jax.ShapeDtypeStruct((width // 2, HALF), t) for t in (F32, BF16, BF16, BF16)],
        in_specs=[SMEM] + [VMEM] * 4,
        out_specs=[VMEM] * 4,
        scratch_shapes=[pltpu.VMEM((2, width, HALF), F32)],
        compiler_params=pltpu.CompilerParams(vmem_limit_bytes=16 << 20),
        cost_estimate=pl.CostEstimate(
            flops=4 * rows * width * width, bytes_accessed=rows * width * 6, transcendentals=0
        ),
        name="local_grad",
    )(rep, high, low, *masked)


def round_kernel(n, spot_ref, *refs):
    held, out_ref, slots = refs[:n], refs[n], refs[n + 1]
    rows = out_ref.shape[0]
    for distance, ref in enumerate(held):
        slots[lax.rem(spot_ref[0] + distance, n)] = ref[ref.shape[0] - rows :, :].astype(F32)
    total = slots[0]
    for i in range(1, n):
        total = total + slots[i]
    out_ref[...] = total.astype(BF16)


def round_sum(spot, held):
    n, shape = len(held), held[0].shape
    return pl.pallas_call(
        functools.partial(round_kernel, n),
        out_shape=jax.ShapeDtypeStruct(shape, BF16),
        in_specs=[SMEM] + [VMEM] * n,
        out_specs=VMEM,
        scratch_shapes=[pltpu.VMEM((n, *shape), F32)],
        compiler_params=pltpu.CompilerParams(vmem_limit_bytes=(2 * n + 8) << 17),
        name="round_sum",
    )(spot, *held)


def whole_kernel(scale, rep_ref, *refs):
    rows = refs[0].shape[0] // 2
    for mask in range(4):
        start = pl.multiple_of(lax.bitwise_xor(rep_ref[0], mask) * rows, rows)
        for h in range(2):
            part = refs[mask][h * rows : (h + 1) * rows, :].astype(F32) * scale
            refs[4][pl.ds(start, rows), h * HALF : (h + 1) * HALF] = part


def whole_grad(rep, quarters, scale):
    size = 2 * quarters[0].shape[0]
    return pl.pallas_call(
        functools.partial(whole_kernel, scale),
        out_shape=jax.ShapeDtypeStruct((size, 2 * HALF), F32),
        in_specs=[SMEM] + [VMEM] * 4,
        out_specs=VMEM,
        compiler_params=pltpu.CompilerParams(vmem_limit_bytes=4 << 20),
        name="whole_grad",
    )(rep, *quarters)


class GradientSum:
    def __init__(self, rep, spot, high, low, masked, n, scale):
        self.rep, self.spot, self.local, self.n, self.scale = rep, spot, (high, low, masked), n, scale
        self.pairs = [[(i, i ^ mask) for i in range(4)] for mask in range(4)]

    def start(self, after):
        high, low, masked = tie(self.local, after)
        self.quarters = local_grad(self.rep, high, low, masked)
        return self.quarters

    def riders(self, after):
        value = self.quarters[0]
        for mask in (1, 2, 3):
            value = value + lax.ppermute(self.quarters[mask], "rep", self.pairs[mask]).astype(F32)
        self.value = value.astype(BF16)
        return self.value

    def finish(self, arrived):
        held = [self.value] + [None] * (self.n - 1)
        for hop, (right, left) in enumerate(arrived, 1):
            held[self.n - hop] = right
            if left is not None:
                held[hop] = left
        value = round_sum(self.spot, held)
        others = [lax.ppermute(value, "rep", self.pairs[mask]) for mask in (1, 2, 3)]
        return whole_grad(self.rep, [value, *others], self.scale)


def on_device(n, features, weight, block_cols, block_vals, out_grad):
    own_rows, width = features.shape
    block = block_vals.shape[-1]
    own_blocks = own_rows // block
    me, layer = lax.axis_index("rows"), lax.axis_index("rep")
    vals = block_vals.reshape(-1, block, block)
    chunks = [features[:, h * HALF : (h + 1) * HALF] for h in range(width // HALF)]
    ready = {}

    def prepared(after):
        my, rep, cols = tie((me.astype(jnp.int32), layer.astype(jnp.int32).reshape(1), block_cols), after)
        cols = cols.reshape(-1)
        back_steps = (ring_place(my, n) - ring_place(cols // own_blocks, n) + n) % n
        ready["spot"] = ring_place(my, n).reshape(1)
        ready["rep"], ready["where"] = rep, back_steps * own_blocks + cols % own_blocks
        ready["vals"] = brought_near(vals)
        return ready["rep"], ready["where"], ready["spot"], ready["vals"]

    numbers = lambda: (ready["where"], ready["rep"], ready["vals"])
    sums, _ = spread(*chunks, n, own_blocks, numbers, SCALE, {"beside": prepared})
    rep = ready["rep"]
    activated, high, low, *masked = middle(rep, weight, out_grad, sums)

    node_total = own_rows * n * 4
    grad = GradientSum(rep, ready["spot"], high, low, masked, n, 1.0 / (SCALE * math.sqrt(node_total)))
    sums, arrived = spread(*masked, n, own_blocks, numbers, None, {"gather 2": grad.start, "riders": grad.riders})
    weight_grad = grad.finish(arrived)
    input_grad = last(weight, sums)
    return activated, input_grad, weight_grad


def solution(mesh):
    placed = (
        P(("rows", "rep"), None),
        P(),
        P("rows", "rep", None),
        P("rows", "rep", None, None, None),
        P("rows", None),
    )
    return jax.shard_map(
        functools.partial(on_device, mesh.shape["rows"]),
        mesh=mesh,
        in_specs=placed,
        out_specs=(P(("rows", "rep"), None), P(("rows", "rep"), None), P()),
        check_vma=False,
    )
```

```python
import functools
import math

import jax
import jax.numpy as jnp
from jax import lax
from jax.experimental import pallas as pl
from jax.experimental.pallas import tpu as pltpu
from jax.sharding import PartitionSpec as P

F32 = jnp.float32
BF16 = jnp.bfloat16
HALF = 128
SCALE = 2.0**-21
VMEM = pl.BlockSpec(memory_space=pltpu.VMEM)
SMEM = pl.BlockSpec(memory_space=pltpu.SMEM)


def ring_order(n):
    return list(range(0, n, 2)) + list(range(n - 1, 0, -2))


def ring_place(i, n):
    return jnp.where(i % 2 == 0, i // 2, n - 1 - i // 2)


def split_dot(left, right, dims):
    high = left.astype(BF16)
    low = (left - high.astype(F32)).astype(BF16)
    out = lax.dot_general(high, right, (dims, ((), ())), preferred_element_type=F32)
    return out + lax.dot_general(low, right, (dims, ((), ())), preferred_element_type=F32)


def tie(arrays, other):
    return lax.optimization_barrier((arrays, other))[0]


def ring_ways(n):
    order = ring_order(n)
    ahead = [(order[i], order[(i + 1) % n]) for i in range(n)]
    return ahead, [(b, a) for a, b in ahead]


def gather_kernel(n, own_blocks, block, scale, where_ref, rep_ref, vals_ref, *refs):
    pieces, (send, keep_far, keep_near, pool) = refs[: n + 1], refs[n + 1 :]
    rows, half = own_blocks * block, n // 2
    starts = [p * rows for p in range(half + 1)] + [half * rows + rows // 2]
    starts += [p * rows for p in range(half + 1, n)]
    for start, ref in zip(starts, pieces):
        piece = ref[: min(ref.shape[0], rows), :]
        pool[start : start + piece.shape[0], :] = piece if scale is None else piece * jnp.asarray(scale, BF16)
    me = rep_ref[0]
    for mask, out, first in ((3, send, 0), (1, send, own_blocks), (2, keep_far, 0), (0, keep_near, 0)):
        base = lax.bitwise_xor(me, mask) * own_blocks
        for j in range(own_blocks):
            total = None
            for s in range(2):
                item = (base + j) * 2 + s
                start = pl.multiple_of(where_ref[item] * block, block)
                term = jnp.dot(vals_ref[item], pool[pl.ds(start, block), :], preferred_element_type=F32)
                total = term if total is None else total + term
            out[(first + j) * block : (first + j + 1) * block, :] = total.astype(out.dtype)


def gather_blocks(where, rep, vals, pieces, n, own_blocks, scale):
    block = vals.shape[-1]
    rows, width = pieces[0].shape
    shapes = [jax.ShapeDtypeStruct((2 * rows, width), BF16)]
    shapes += [jax.ShapeDtypeStruct((rows, width), F32)] * 2
    size = vals.size * 2 + 2 * n * rows * width * 2 + rows * width * 12
    return pl.pallas_call(
        functools.partial(gather_kernel, n, own_blocks, block, scale),
        out_shape=shapes,
        in_specs=[SMEM, SMEM, VMEM] + [VMEM] * (n + 1),
        out_specs=[VMEM] * 3,
        scratch_shapes=[pltpu.VMEM((n * rows, width), BF16)],
        compiler_params=pltpu.CompilerParams(vmem_limit_bytes=size + (8 << 20)),
        cost_estimate=pl.CostEstimate(
            flops=200 * vals.size * width, bytes_accessed=size, transcendentals=0
        ),
        name="gather_blocks",
    )(where, rep, vals, *pieces)


def scatter_kernel(own_blocks, block, scale, where_ref, rep_ref, vals_ref, *refs):
    sources, (own_ref, out_ref, ahead_ref, behind_ref) = refs[:4], refs[4:]
    rows = own_blocks * block
    out_ref[...] = jnp.zeros_like(out_ref)
    me = rep_ref[0]
    for mask in range(4):
        base = lax.bitwise_xor(me, mask) * own_blocks
        for j in range(own_blocks):
            source = sources[mask][j * block : (j + 1) * block, :]
            if scale is not None:
                source = source * jnp.asarray(scale, BF16)
            for s in range(2):
                item = (base + j) * 2 + s
                start = pl.multiple_of(where_ref[item] * block, block)
                term = lax.dot_general(vals_ref[item], source, (((0,), (0,)), ((), ())), preferred_element_type=F32)
                out_ref[pl.ds(start, block), :] += term
    own_ref[...] = out_ref[:rows, :]
    first, mid = out_ref.shape[0] // 2, rows // 2
    ahead_ref[...] = out_ref[first : first + mid, :].astype(ahead_ref.dtype)
    behind_ref[...] = out_ref[first + mid : first + rows, :].astype(behind_ref.dtype)


def scatter_blocks(where, rep, vals, sources, n, own_blocks, scale, sent):
    block = vals.shape[-1]
    rows, width = sources[0].shape
    size = vals.size * 2 + 4 * rows * width * 2 + (n + 1) * rows * width * 4
    return pl.pallas_call(
        functools.partial(scatter_kernel, own_blocks, block, scale),
        out_shape=[jax.ShapeDtypeStruct((size_of * rows, width), F32) for size_of in (1, n)]
        + [jax.ShapeDtypeStruct((rows // 2, width), sent)] * 2,
        in_specs=[SMEM, SMEM, VMEM] + [VMEM] * 4,
        out_specs=[VMEM] * 4,
        compiler_params=pltpu.CompilerParams(vmem_limit_bytes=size + (4 << 20)),
        cost_estimate=pl.CostEstimate(
            flops=2 * vals.size * width, bytes_accessed=size, transcendentals=0
        ),
        name="scatter_blocks",
    )(where, rep, vals, *sources)


def near_kernel(vals_ref, out_ref, sem):
    copy = pltpu.make_async_copy(vals_ref, out_ref, sem)
    copy.start()
    copy.wait()


def brought_near(vals):
    return pl.pallas_call(
        near_kernel,
        out_shape=jax.ShapeDtypeStruct(vals.shape, vals.dtype),
        in_specs=[pl.BlockSpec(memory_space=pl.ANY)],
        out_specs=VMEM,
        scratch_shapes=[pltpu.SemaphoreType.DMA],
        compiler_params=pltpu.CompilerParams(vmem_limit_bytes=4 << 20),
        name="brought_near",
    )(vals)


def add_terms(pair, terms, sent, riders):
    rows = terms[0].shape[0]
    mid = rows // 2
    size = pair[0].shape[0] - riders
    right, left = (array[:size].astype(F32) for array in pair)
    if size == mid:
        right = jnp.concatenate([terms[0][:mid] + right, terms[0][mid:]], 0)
        left = jnp.concatenate([terms[1][:mid], terms[1][mid:] + left], 0)
    else:
        right, left = terms[0] + right, terms[1] + left
    return tuple(
        jnp.concatenate([array.astype(sent), came[size:]], 0) if riders else array.astype(sent)
        for array, came in zip((right, left), pair)
    )


def spread(first, second, n, own_blocks, numbers, scale, hooks):
    ahead, behind = ring_ways(n)
    rows, half = first.shape[0], n // 2
    mid = rows // 2
    sent = BF16 if n <= 8 else F32
    pairs = [[(i, i ^ mask) for i in range(4)] for mask in range(4)]
    hook = lambda name, after: hooks[name](after) if name in hooks else ()
    step = lambda pair: (lax.ppermute(pair[0], "rows", ahead), lax.ppermute(pair[1], "rows", behind))

    across = lax.ppermute(second, "rep", pairs[2])
    beside = lax.ppermute(tie(second, hook("beside", ())), "rep", pairs[1])
    gathered = step((first, first))
    pieces = [first] + [None] * n
    pieces[1], pieces[n] = gathered
    moving, riders, arrived = None, 0, []
    for hop in range(2, half + 1):
        if hop == 2:
            gathered = tie(gathered, (across, hook("gather 2", across)))
            far = lax.ppermute(across, "rep", pairs[1])
        else:
            gathered = tie(gathered, (moving, hook("gather %d" % hop, moving)))
        if hop == half:
            gathered = gathered[0][:mid], gathered[1][mid:rows]
        elif riders:
            gathered = tuple(jnp.concatenate([array[:rows], rider.astype(array.dtype)], 0) for array in gathered)
        behind_it = gathered
        gathered = step(gathered)
        pieces[hop], pieces[n + 1 - hop] = gathered
        if hop == 2:
            where, rep, vals = numbers()
            sources = tie([second, beside, across, far], behind_it)
            own, partial, *moving = scatter_blocks(where, rep, vals, sources, n, own_blocks, scale, sent)
            term = lambda distance: partial[distance * rows : (distance + 1) * rows]
            moving = tuple(moving)
            if "riders" in hooks:
                rider = hooks["riders"](behind_it).astype(sent)
                riders = rider.shape[0]
                moving = tuple(jnp.concatenate([array, rider], 0) for array in moving)
        else:
            came = step(moving)
            arrived.append(came)
            moving = add_terms(came, (term(half + hop - 2), term(half - hop + 2)), sent, riders)
            moving = tie(moving, behind_it)
    pieces = tie(pieces, moving)
    *summed, crossing = reduce_rep(gather_blocks(where, rep, vals, pieces, n, own_blocks, scale))
    came = step(moving)
    arrived.append(came)
    moving = add_terms([array[:rows] for array in came], (term(n - 1), term(1)), sent, 0)
    if riders:
        moving = jnp.concatenate([moving[0], came[0][rows:]], 0), moving[1]
    moving = tie(moving, crossing)
    right, left = step(moving)
    arrived.append((right, None))
    return [*summed, own, right, left], arrived


def reduce_rep(parts):
    send, keep_far, keep_near = parts
    got = lax.ppermute(send, "rep", [(i, i ^ 1) for i in range(4)])
    crossing = (keep_far + got[: keep_far.shape[0]].astype(F32)).astype(BF16)
    return keep_near, got, lax.ppermute(crossing, "rep", [(i, i ^ 2) for i in range(4)]), crossing


def joined(refs):
    near, got, cross, own, right, left = refs
    rows = near.shape[0]
    first = near[...] + got[rows:, :].astype(F32) + cross[...].astype(F32)
    second = own[...] + (right[:rows, :].astype(F32) + left[...].astype(F32))
    return jnp.concatenate([first, second], axis=1)


def middle_kernel(rep_ref, weight_ref, grad_ref, *refs):
    sums, (act_ref, high_ref, low_ref, *masked_refs, grad, sem) = refs[:6], refs[6:]
    rows = act_ref.shape[0]
    start = pl.multiple_of(rep_ref[0] * rows, rows)
    copy = pltpu.make_async_copy(grad_ref.at[pl.ds(start, rows), :], grad, sem)
    copy.start()
    held = joined(sums)
    high = held.astype(BF16)
    low = (held - high.astype(F32)).astype(BF16)
    high_ref[...] = high
    low_ref[...] = low
    weight = weight_ref[...]
    summed = jnp.dot(high, weight, preferred_element_type=F32)
    summed = (summed + jnp.dot(low, weight, preferred_element_type=F32)) * (1.0 / SCALE)
    gate = jax.nn.sigmoid(summed)
    act_ref[...] = (summed * gate).astype(BF16)
    slope = gate * (1.0 + summed * (1.0 - gate))
    copy.wait()
    masked = (grad[...].astype(F32) * slope).astype(BF16)
    for h, ref in enumerate(masked_refs):
        ref[...] = masked[:, h * HALF : (h + 1) * HALF]


def middle(rep, weight, grad, sums):
    rows, width = sums[0].shape[0], grad.shape[1]
    shapes = [jax.ShapeDtypeStruct((rows, width), BF16)] * 3
    shapes += [jax.ShapeDtypeStruct((rows, HALF), BF16)] * (width // HALF)
    return pl.pallas_call(
        middle_kernel,
        out_shape=shapes,
        in_specs=[SMEM, VMEM, pl.BlockSpec(memory_space=pl.ANY)] + [VMEM] * 6,
        out_specs=[VMEM] * len(shapes),
        scratch_shapes=[pltpu.VMEM((rows, width), BF16), pltpu.SemaphoreType.DMA],
        compiler_params=pltpu.CompilerParams(vmem_limit_bytes=16 << 20),
        cost_estimate=pl.CostEstimate(
            flops=4 * rows * width * width, bytes_accessed=rows * width * 18, transcendentals=rows * width
        ),
        name="middle",
    )(rep, weight, grad, *sums)


def last_kernel(weight_ref, *refs):
    back = joined(refs[:6])
    refs[6][...] = split_dot(back, weight_ref[...], ((1,), (1,))).astype(BF16)


def last(weight, sums):
    rows, width = sums[0].shape[0], weight.shape[0]
    return pl.pallas_call(
        last_kernel,
        out_shape=jax.ShapeDtypeStruct((rows, width), BF16),
        in_specs=[VMEM] * 7,
        out_specs=VMEM,
        compiler_params=pltpu.CompilerParams(vmem_limit_bytes=24 << 20),
        cost_estimate=pl.CostEstimate(
            flops=4 * rows * width * width, bytes_accessed=rows * width * 14, transcendentals=0
        ),
        name="last",
    )(weight, *sums)


def local_kernel(rep_ref, high_ref, low_ref, *refs):
    masked, outs = refs[:2], refs[2:6]
    total = refs[6]
    for h, ref in enumerate(masked):
        part = None
        for held in (high_ref, low_ref):
            term = lax.dot_general(held[...], ref[...], (((0,), (0,)), ((), ())), preferred_element_type=F32)
            part = term if part is None else part + term
        total[h] = part
    rows = outs[0].shape[0] // 2
    for mask, out in enumerate(outs):
        start = pl.multiple_of(lax.bitwise_xor(rep_ref[0], mask) * rows, rows)
        for h in range(2):
            out[h * rows : (h + 1) * rows, :] = total[h, pl.ds(start, rows), :].astype(out.dtype)


def local_grad(rep, high, low, masked):
    rows, width = high.shape
    return pl.pallas_call(
        local_kernel,
        out_shape=[jax.ShapeDtypeStruct((width // 2, HALF), t) for t in (F32, BF16, BF16, BF16)],
        in_specs=[SMEM] + [VMEM] * 4,
        out_specs=[VMEM] * 4,
        scratch_shapes=[pltpu.VMEM((2, width, HALF), F32)],
        compiler_params=pltpu.CompilerParams(vmem_limit_bytes=16 << 20),
        cost_estimate=pl.CostEstimate(
            flops=4 * rows * width * width, bytes_accessed=rows * width * 6, transcendentals=0
        ),
        name="local_grad",
    )(rep, high, low, *masked)


def round_kernel(n, spot_ref, *refs):
    held, out_ref, slots = refs[:n], refs[n], refs[n + 1]
    rows = out_ref.shape[0]
    for distance, ref in enumerate(held):
        slots[lax.rem(spot_ref[0] + distance, n)] = ref[ref.shape[0] - rows :, :].astype(F32)
    total = slots[0]
    for i in range(1, n):
        total = total + slots[i]
    out_ref[...] = total.astype(BF16)


def round_sum(spot, held):
    n, shape = len(held), held[0].shape
    return pl.pallas_call(
        functools.partial(round_kernel, n),
        out_shape=jax.ShapeDtypeStruct(shape, BF16),
        in_specs=[SMEM] + [VMEM] * n,
        out_specs=VMEM,
        scratch_shapes=[pltpu.VMEM((n, *shape), F32)],
        compiler_params=pltpu.CompilerParams(vmem_limit_bytes=(2 * n + 8) << 17),
        name="round_sum",
    )(spot, *held)


def whole_kernel(scale, rep_ref, *refs):
    rows = refs[0].shape[0] // 2
    for mask in range(4):
        start = pl.multiple_of(lax.bitwise_xor(rep_ref[0], mask) * rows, rows)
        for h in range(2):
            part = refs[mask][h * rows : (h + 1) * rows, :].astype(F32) * scale
            refs[4][pl.ds(start, rows), h * HALF : (h + 1) * HALF] = part


def whole_grad(rep, quarters, scale):
    size = 2 * quarters[0].shape[0]
    return pl.pallas_call(
        functools.partial(whole_kernel, scale),
        out_shape=jax.ShapeDtypeStruct((size, 2 * HALF), F32),
        in_specs=[SMEM] + [VMEM] * 4,
        out_specs=VMEM,
        compiler_params=pltpu.CompilerParams(vmem_limit_bytes=4 << 20),
        name="whole_grad",
    )(rep, *quarters)


class GradientSum:
    def __init__(self, rep, spot, high, low, masked, n, scale):
        self.rep, self.spot, self.local, self.n, self.scale = rep, spot, (high, low, masked), n, scale
        self.pairs = [[(i, i ^ mask) for i in range(4)] for mask in range(4)]

    def start(self, after):
        high, low, masked = tie(self.local, after)
        self.quarters = local_grad(self.rep, high, low, masked)
        return self.quarters

    def riders(self, after):
        value = self.quarters[0]
        for mask in (1, 2, 3):
            value = value + lax.ppermute(self.quarters[mask], "rep", self.pairs[mask]).astype(F32)
        self.value = value.astype(BF16)
        return self.value

    def finish(self, arrived):
        held = [self.value] + [None] * (self.n - 1)
        for hop, (right, left) in enumerate(arrived, 1):
            held[self.n - hop] = right
            if left is not None:
                held[hop] = left
        value = round_sum(self.spot, held)
        others = [lax.ppermute(value, "rep", self.pairs[mask]) for mask in (1, 2, 3)]
        return whole_grad(self.rep, [value, *others], self.scale)


def on_device(n, features, weight, block_cols, block_vals, out_grad):
    own_rows, width = features.shape
    block = block_vals.shape[-1]
    own_blocks = own_rows // block
    me, layer = lax.axis_index("rows"), lax.axis_index("rep")
    vals = block_vals.reshape(-1, block, block)
    chunks = [features[:, h * HALF : (h + 1) * HALF] for h in range(width // HALF)]
    ready = {}

    def prepared(after):
        my, rep, cols = tie((me.astype(jnp.int32), layer.astype(jnp.int32).reshape(1), block_cols), after)
        cols = cols.reshape(-1)
        back_steps = (ring_place(my, n) - ring_place(cols // own_blocks, n) + n) % n
        ready["spot"] = ring_place(my, n).reshape(1)
        ready["rep"], ready["where"] = rep, back_steps * own_blocks + cols % own_blocks
        ready["vals"] = brought_near(vals)
        return ready["rep"], ready["where"], ready["spot"], ready["vals"]

    numbers = lambda: (ready["where"], ready["rep"], ready["vals"])
    sums, _ = spread(*chunks, n, own_blocks, numbers, SCALE, {"beside": prepared})
    rep = ready["rep"]
    activated, high, low, *masked = middle(rep, weight, out_grad, sums)

    node_total = own_rows * n * 4
    grad = GradientSum(rep, ready["spot"], high, low, masked, n, 1.0 / (SCALE * math.sqrt(node_total)))
    sums, arrived = spread(*masked, n, own_blocks, numbers, None, {"gather 2": grad.start, "riders": grad.riders})
    weight_grad = grad.finish(arrived)
    input_grad = last(weight, sums)
    return activated, input_grad, weight_grad


def solution(mesh):
    placed = (
        P(("rows", "rep"), None),
        P(),
        P("rows", "rep", None),
        P("rows", "rep", None, None, None),
        P("rows", None),
    )
    return jax.shard_map(
        functools.partial(on_device, mesh.shape["rows"]),
        mesh=mesh,
        in_specs=placed,
        out_specs=(P(("rows", "rep"), None), P(("rows", "rep"), None), P()),
        check_vma=False,
    )
```
